32 devices in a mesh: role: 2 (over y), dev: 16 (over z, x, core).
Axes of the slice: x: 2, y: 2, z: 4, core: 2. Of those that a mesh axis runs over, the one named last changes fastest.
Arguments:
- features: bfloat16 [2, 32, 32, 64, 128], P('role', None, 'dev'), may hold values from -6 to 6
- labels: bfloat16 [2, 32, 64, 128], P('role', 'dev'), may hold values from 0 to 1
- crop_block: int32 [2, 16, 16], P('role'), may hold values from -1 to 15, as said below
- weight: float32 [64, 864], P('dev'), may hold values from -0.21875 to 0.21875
- gain: float32 [64], P('dev'), may hold values from 0.1 to 1.9
- shift: float32 [64], P('dev'), may hold values from -3 to 3
- head: float32 [64], P('dev'), may hold values from -1.5 to 1.5
- run_mean: float32 [64], P('dev'), may hold values from -2 to 2
- run_var: float32 [64], P('dev'), may hold values from 0.5 to 2
Outputs:
- scores: float32 [2, 32, 64, 128], P('role', 'dev')
- weight_grad: float32 [64, 864], P('dev')
- vector_grad: float32 [64, 3], P('dev')
The draws below stay inside these ranges and needn't reach their ends.
Inputs may be any that keep to these rules, and one draw needn't show every extreme that they name: crop_block[g, s, t] >= 0 is the row block b that source s of group g sends to learner t; -1 means no crop. Source s always sends to learner s, and to between 4 and 12 learners in all.
All inputs are finite; a program needn't handle non-finite values.
Results may differ from the reference program's by a relative error of at most 0.002.
The reference program's roundings to bfloat16 on the way count: a program that leaves them out, or rounds other values in their place, can miss the bound.
Values may be sent and summed in bfloat16 or wider, within the bound.
A program may use at most 128 MiB of HBM per device.

```python
import math
import jax
import jax.numpy as jnp
from jax import lax

CI = 32
CO = 64
ZD = 2
YS = 64
XS = 128
CY = 4
Z = 32
N_ROLE = 2
N_DEV = 16


def draw_crop_block(key, part):
    subkeys = jax.random.split(jax.random.fold_in(key, 17), 3)
    counts = jax.random.randint(subkeys[0], (N_ROLE, N_DEV, 1), N_DEV // 4, 3 * N_DEV // 4 + 1)
    offsets = jnp.arange(N_DEV)
    scores = jax.random.randint(subkeys[1], (N_ROLE, N_DEV, N_DEV), 0, 1 << 20) * N_DEV + offsets
    scores = jnp.where(offsets == 0, -1, scores)
    ranking = jnp.sum((scores[..., None, :] < scores[..., :, None]).astype(jnp.int32), axis=-1)
    chosen = ranking < counts
    distance = (offsets[None, :] - offsets[:, None]) % N_DEV
    distance = jnp.broadcast_to(distance, (N_ROLE, N_DEV, N_DEV)).astype(jnp.int32)
    picked = jnp.take_along_axis(chosen, distance, axis=2)
    blocks = jax.random.randint(subkeys[2], (N_ROLE, N_DEV, N_DEV), 0, YS // CY)
    return jnp.where(picked, blocks, -1).astype(jnp.int32)


def block_scale(stream_key, shape, cuts, least, largest):
    def one(dim, blocks):
        draws = jax.random.uniform(jax.random.fold_in(jax.random.fold_in(stream_key, 6), dim), (blocks,), jnp.float32, least / len(cuts), largest / len(cuts))
        return jnp.repeat(jnp.exp(draws), shape[dim] // blocks).reshape((-1,) + (1,) * (len(shape) - dim - 1))

    factor_of = one(*cuts[0])
    for cut in cuts[1:]:
        factor_of = factor_of * one(*cut)
    return factor_of


def bell_draw(stream_key, shape, spread, reach, shards=(), kind=jnp.bfloat16):
    entries = jax.random.normal(stream_key, shape, jnp.float32) * spread
    if len(shards) > 0:
        entries = block_scale(stream_key, shape, shards, -0.22, 0.18) * entries
    return jnp.clip(entries, min=-reach, max=reach).astype(kind)


def setup_inputs(seed: int = 0) -> dict:
    splits = jax.random.split(jax.random.key(seed), 10)
    features = bell_draw(splits[0], (N_ROLE, CI, Z, YS, XS), 1.0, 6.0, ((0, 2), (2, 16)))
    labels = jnp.clip(1.0 * jax.random.uniform(splits[1], (N_ROLE, Z, YS, XS), jnp.float32) ** block_scale(splits[1], (N_ROLE, Z, YS, XS), ((0, 2), (1, 16)), -0.2, 0.2), 0.0, 1.0).astype(jnp.bfloat16)
    crop_block = draw_crop_block(jax.random.fold_in(splits[9], 71), 0)
    weight = bell_draw(splits[3], (CO, 27 * CI), (27 * CI) ** -0.5, 0.21875, ((0, 16),), jnp.float32)
    gain = jnp.clip(1.0 + 0.18 * jax.random.normal(splits[4], (CO,), jnp.float32), 0.1, 1.9)
    shift = bell_draw(splits[5], (CO,), 0.5, 3.0, ((0, 16),), jnp.float32)
    head = bell_draw(splits[6], (CO,), 0.25, 1.5, ((0, 16),), jnp.float32)
    run_mean = bell_draw(splits[7], (CO,), 0.3, 2.0, ((0, 16),), jnp.float32)
    run_var = jnp.clip(jnp.exp(math.log(2.0) - 1.3862944 * jax.random.uniform(splits[8], (CO,), jnp.float32) ** block_scale(splits[8], (CO,), ((0, 16),), -0.2, 0.2)), 0.5, 2.0)
    return {"features": features, "labels": labels, "crop_block": crop_block, "weight": weight, "gain": gain, "shift": shift, "head": head, "run_mean": run_mean, "run_var": run_var}


epsilon = 1e-05

def conv_field(field, weight_matrix):
    filter_weight = weight_matrix.astype(jnp.float32).reshape(CO, 3, 3, 3, CI).transpose(0, 4, 1, 2, 3)
    return lax.conv_general_dilated(field.astype(jnp.float32), filter_weight, (1, 1, 1), ((1, 1), (1, 1), (1, 1)), dimension_numbers=('NCDHW', 'OIDHW', 'NCDHW'), precision=lax.Precision.HIGHEST)

def reference(features, labels, crop_block, weight, gain, shift, head, run_mean, run_var):
    weight_f = lax.optimization_barrier(weight.astype(jnp.bfloat16)).astype(jnp.float32)
    stacked = jnp.stack([gain, shift, head, run_mean, run_var]).astype(jnp.bfloat16)
    vector_f = lax.optimization_barrier(stacked).astype(jnp.float32)
    gain_value = vector_f[0]
    shift_value = vector_f[1]
    head_value = vector_f[2]
    mean_value = vector_f[3]
    spread_value = vector_f[4]
    block_count = YS // CY
    crop_cells = ZD * CY * XS
    sources = jnp.arange(N_DEV)
    score_list = []
    weight_total = jnp.zeros((CO, 27 * CI), jnp.float32)
    vector_total = jnp.zeros((CO, 3), jnp.float32)
    for group_index in range(N_ROLE):
        grouped_feature_field = features[group_index]
        conv_whole = conv_field(grouped_feature_field[None], weight_f)[0]
        normed = (conv_whole - mean_value[:, None, None, None]) * lax.rsqrt(spread_value + epsilon)[:, None, None, None]
        hidden = jax.nn.relu(gain_value[:, None, None, None] * normed + shift_value[:, None, None, None])
        score_list.append(jnp.einsum('c,czyx->zyx', head_value, hidden, precision=lax.Precision.HIGHEST))
        pieces = grouped_feature_field.reshape(CI, N_DEV, ZD, block_count, CY, XS).transpose(1, 3, 0, 2, 4, 5)
        pieces = pieces.reshape(N_DEV * block_count, CI, ZD, CY, XS)
        crop_out = conv_field(pieces, weight_f).astype(jnp.bfloat16).reshape(N_DEV, block_count, CO, ZD, CY, XS)
        label_blocks = labels[group_index].reshape(N_DEV, ZD, block_count, CY, XS).transpose(0, 2, 1, 3, 4)

        def learner(running, column):
            live_flags = column >= 0
            chosen = jnp.maximum(column, 0).astype(jnp.int32)
            ufield = crop_out[sources, chosen].astype(jnp.float32)
            target = label_blocks[sources, chosen].astype(jnp.float32)
            live_weights = live_flags.astype(jnp.float32)
            cell_count = jnp.sum(live_weights) * crop_cells
            mask = live_weights[:, None, None, None, None]

            def loss_fn(field_in, gain_in, shift_in, head_input_channels):
                channel_mean = lax.optimization_barrier(jnp.sum(field_in * mask, axis=(0, 2, 3, 4))) / cell_count
                centred = field_in - channel_mean[None, :, None, None, None]
                channel_var = lax.optimization_barrier(jnp.sum((centred * mask) ** 2, axis=(0, 2, 3, 4))) / cell_count
                normal = centred * lax.rsqrt(channel_var + epsilon)[None, :, None, None, None]
                hidden_width = jax.nn.relu(gain_in[None, :, None, None, None] * normal + shift_in[None, :, None, None, None])
                ranked_crops = jnp.einsum('bjnkw,j->bnkw', hidden_width, head_input_channels, precision=lax.Precision.HIGHEST)
                return 0.5 * jnp.sum(live_weights[:, None, None, None] * (ranked_crops - target) ** 2) / cell_count
            loss_value, pull = jax.vjp(loss_fn, ufield, gain_value, shift_value, head_value)
            dfield, dgain, dshift, dhead = pull(jnp.ones_like(loss_value))
            dfield = lax.optimization_barrier(dfield.astype(jnp.bfloat16)).astype(jnp.float32)
            grads_sum, vector_sum = running
            grads_sum = grads_sum.at[sources, chosen].add(dfield * mask)
            vector_sum = vector_sum + jnp.stack([dgain, dshift, dhead], 1)
            return ((grads_sum, vector_sum), None)
        initial = (jnp.zeros((N_DEV, block_count, CO, ZD, CY, XS), jnp.float32), jnp.zeros((CO, 3), jnp.float32))
        (grads_sum, vector_sum), _ = lax.scan(learner, initial, crop_block[group_index].T)
        _, pull_weight = jax.vjp(lambda kernel_matrix: conv_field(pieces, kernel_matrix), weight_f)
        weight_part, = pull_weight(grads_sum.reshape(N_DEV * block_count, CO, ZD, CY, XS))
        weight_total = weight_total + weight_part
        vector_total = vector_total + vector_sum
    return (jnp.stack(score_list), weight_total, vector_total)
```

```python
import functools

import jax
import jax.numpy as jnp
from jax import lax
from jax.experimental import pallas as pl
from jax.experimental.pallas import tpu as pltpu
from jax.sharding import PartitionSpec as P

CY = 4
EPS = 1e-05
LANES = 128
F32 = jnp.float32
BF16 = jnp.bfloat16


def shift_lanes(value, offset):
    lane = lax.broadcasted_iota(jnp.int32, value.shape, 1)
    width = value.shape[1]
    if offset < 0:
        return jnp.where(lane == 0, 0.0, pltpu.roll(value, 1, 1))
    return jnp.where(lane == width - 1, 0.0, pltpu.roll(value, width - 1, 1))


def column(table, index):
    lane = lax.broadcasted_iota(jnp.int32, table.shape, 1)
    return jnp.sum(jnp.where(lane == index, table, 0.0), axis=1, keepdims=True)


def put_column(ref, rows, index, value):
    part = ref[rows, :]
    lane = lax.broadcasted_iota(jnp.int32, part.shape, 1)
    ref[rows, :] = jnp.where(lane == index, value, part)


def crop_tiles(planes, block, channels):
    for z in range(planes):
        for y in range(CY):
            cell_row = z * CY + y
            for dz in range(3):
                for dy in range(3):
                    zs, ys = z + dz - 1, y + dy - 1
                    if 0 <= zs < planes and 0 <= ys < CY:
                        yield (dz * 3 + dy) * channels, cell_row, zs, ys


def fill_patches(patch_ref, slab_ref, block, planes, channels, columns):
    base = pl.multiple_of((block * CY + 1) * channels, channels)
    for tap_row, cell_row, zs, ys in crop_tiles(planes, block, channels):
        patch_ref[pl.ds(tap_row, channels), pl.ds(cell_row * columns, columns)] = slab_ref[
            zs, pl.ds(base + ys * channels, channels), :
        ]


def conv_rows(weights, patch_ref, first, rows, out_channels, columns):
    taps = jnp.dot(
        weights,
        patch_ref[:, first * columns : (first + rows) * columns],
        preferred_element_type=F32,
    )
    results = []
    for row in range(rows):
        part = taps[:, row * columns : (row + 1) * columns]
        results.append(
            part[out_channels : 2 * out_channels]
            + shift_lanes(part[:out_channels], -1)
            + shift_lanes(part[2 * out_channels :], 1)
        )
    return results


def forward_kernel(dims, route_ref, param_ref, slab_ref, u_ref, stat_ref, patch, table, turned):
    planes, blocks, channels, out_channels, columns, slots = dims
    cell_rows = planes * CY
    cells = cell_rows * columns
    patch[...] = jnp.zeros_like(patch)
    table[...] = jnp.zeros_like(table)

    def step(block, carry):
        fill_patches(patch, slab_ref, block, planes, channels, columns)
        weights = param_ref[0 : 3 * out_channels, :]
        total = jnp.zeros((out_channels, columns), F32)
        for first in range(0, cell_rows, 2):
            rows = conv_rows(weights, patch, first, 2, out_channels, columns)
            for k, row in enumerate(rows):
                rounded = row.astype(BF16)
                u_ref[block, :, (first + k) * columns : (first + k + 1) * columns] = rounded
                total = total + rounded.astype(F32)
        total = jnp.sum(total, axis=1, keepdims=True)
        mean = total * (1.0 / cells)
        square = jnp.zeros((out_channels, columns), F32)
        for row in range(cell_rows):
            diff = u_ref[block, :, row * columns : (row + 1) * columns].astype(F32) - mean
            square = square + diff * diff
        square = jnp.sum(square, axis=1, keepdims=True)
        put_column(table, slice(0, out_channels), block, total)
        put_column(table, slice(out_channels, 2 * out_channels), block, square)
        return carry

    lax.fori_loop(0, blocks, step, 0)
    turned[...] = jnp.transpose(table[...])

    def route(slot, carry):
        block = route_ref[slot]
        entry = turned[pl.ds(jnp.maximum(block, 0), 1), :]
        stat_ref[pl.ds(slot, 1), :] = jnp.where(block >= 0, entry, 0.0)
        return carry

    lax.fori_loop(0, slots, route, 0)


def score_kernel(dims, param_ref, slab_ref, low_ref, high_ref, out_ref, patch):
    planes, blocks, channels, out_channels, columns, slots = dims
    height = blocks * CY
    group = 8
    taps = 3 * channels
    vectors = param_ref[3 * out_channels :, :LANES].astype(F32)
    gain, shift, head, mean, spread = (vectors[:, k : k + 1] for k in range(5))
    inverse = lax.rsqrt(spread + EPS)

    for z in range(planes):

        def step(number, carry, z=z):
            for row in range(group):
                start = pl.multiple_of((number * group + row) * channels, channels)
                for dz in range(3):
                    zs = z + dz - 1
                    where = pl.ds(start, taps)
                    if zs < 0:
                        piece = low_ref[where, :]
                    elif zs >= planes:
                        piece = high_ref[where, :]
                    else:
                        piece = slab_ref[zs, where, :]
                    patch[dz * taps : (dz + 1) * taps, row * columns : (row + 1) * columns] = piece
            weights = param_ref[0 : 3 * out_channels, :]
            lines = []
            for first in range(0, group, 2):
                for value in conv_rows(weights, patch, first, 2, out_channels, columns):
                    hidden = jnp.maximum(gain * ((value - mean) * inverse) + shift, 0.0)
                    lines.append(jnp.sum(head * hidden, axis=0, keepdims=True))
            out_ref[z, pl.ds(pl.multiple_of(number * group, group), group), :] = jnp.concatenate(
                lines, axis=0
            )
            return carry

        lax.fori_loop(0, height // group, step, 0)


def crop_row(u_ref, label_ref, block, row, columns, mu, inverse, vectors, count):
    gain, shift, head = vectors
    value = u_ref[block, :, row * columns : (row + 1) * columns].astype(F32)
    normal = (value - mu) * inverse
    before = gain * normal + shift
    hidden = jnp.maximum(before, 0.0)
    score = jnp.sum(head * hidden, axis=0, keepdims=True)
    residual = (score - label_ref[block, row : row + 1, :]) / count
    dbefore = jnp.where(before > 0, head * residual, 0.0)
    return normal, hidden, residual, dbefore


def sums_kernel(
    dims,
    route_ref,
    count_ref,
    param_ref,
    u_ref,
    label_ref,
    stat_ref,
    live_ref,
    counts_ref,
    sum_ref,
    norm_ref,
    vec_ref,
    square,
    table,
):
    planes, blocks, channels, out_channels, columns, slots = dims
    cell_rows = planes * CY
    cells = cell_rows * columns
    sources = stat_ref.shape[0]
    total = stat_ref[0]
    for s in range(1, sources):
        total = total + stat_ref[s]
    counts = counts_ref[...]
    mu = total / counts
    spread = jnp.zeros_like(mu)
    for s in range(sources):
        entry = stat_ref[s]
        diff = entry * (1.0 / cells) - mu
        spread = spread + (
            pltpu.roll(entry, LANES - out_channels, 1) + live_ref[s] * cells * (diff * diff)
        )
    inverse = lax.rsqrt(spread / counts + EPS)
    lane = lax.broadcasted_iota(jnp.int32, mu.shape, 1)
    square[...] = jnp.zeros_like(square)
    square[0:slots, :] = jnp.where(lane < out_channels, mu, pltpu.roll(inverse, out_channels, 1))
    norm_ref[...] = jnp.transpose(square[...])
    table[...] = jnp.zeros_like(table)
    vec_ref[...] = jnp.zeros_like(vec_ref)

    def step(slot, carry):
        block = route_ref[slot]

        @pl.when(block >= 0)
        def _():
            vec = param_ref[3 * out_channels :, :LANES].astype(F32)
            vectors = tuple(vec[:, k : k + 1] for k in range(3))
            pair = column(norm_ref[...], slot)
            mean, inv = pair[:out_channels], pair[out_channels:]
            count = count_ref[slot]
            first = jnp.zeros((out_channels, columns), F32)
            second, third = first, first
            for row in range(cell_rows):
                normal, hidden, residual, dbefore = crop_row(
                    u_ref, label_ref, block, row, columns, mean, inv, vectors, count
                )
                first = first + dbefore
                second = second + dbefore * normal
                third = third + hidden * residual
            put_column(
                table, slice(0, out_channels), slot, jnp.sum(first, axis=1, keepdims=True)
            )
            put_column(
                table,
                slice(out_channels, 2 * out_channels),
                slot,
                jnp.sum(second, axis=1, keepdims=True),
            )
            vec_ref[...] += third

        return carry

    lax.fori_loop(0, slots, step, 0)
    both = table[...]
    sums = jnp.sum(both, axis=1, keepdims=True)
    last = jnp.sum(vec_ref[...], axis=1, keepdims=True)
    wide = lax.broadcasted_iota(jnp.int32, vec_ref.shape, 1)
    vec_ref[...] = jnp.where(
        wide == 0,
        sums[out_channels:],
        jnp.where(wide == 1, sums[:out_channels], jnp.where(wide == 2, last, 0.0)),
    )
    square[...] = jnp.transpose(both)
    sum_ref[...] = square[0:slots, :]


def grad_kernel(
    dims,
    route_ref,
    count_ref,
    param_ref,
    slab_ref,
    u_ref,
    label_ref,
    sum_ref,
    counts_ref,
    norm_ref,
    grad_ref,
    patch,
    field,
    square,
    means,
):
    planes, blocks, channels, out_channels, columns, slots = dims
    cell_rows = planes * CY
    total = sum_ref[0]
    for s in range(1, sum_ref.shape[0]):
        total = total + sum_ref[s]
    square[...] = jnp.zeros_like(square)
    square[0:slots, :] = total / counts_ref[...]
    means[...] = jnp.transpose(square[...])
    patch[...] = jnp.zeros_like(patch)
    grad_ref[...] = jnp.zeros_like(grad_ref)

    def step(slot, carry):
        block = route_ref[slot]

        @pl.when(block >= 0)
        def _():
            vec = param_ref[3 * out_channels :, :LANES].astype(F32)
            vectors = tuple(vec[:, k : k + 1] for k in range(3))
            gain = vectors[0]
            pair = column(norm_ref[...], slot)
            mean, inv = pair[:out_channels], pair[out_channels:]
            pair = column(means[...], slot)
            first, second = gain * pair[:out_channels], gain * pair[out_channels:]
            count = count_ref[slot]
            fill_patches(patch, slab_ref, block, planes, channels, columns)
            for row in range(cell_rows):
                normal, hidden, residual, dbefore = crop_row(
                    u_ref, label_ref, block, row, columns, mean, inv, vectors, count
                )
                du = inv * (dbefore * gain - first - normal * second)
                du = du.astype(BF16).astype(F32)
                where = slice(row * columns, (row + 1) * columns)
                field[0:out_channels, where] = shift_lanes(du, 1).astype(BF16)
                field[out_channels : 2 * out_channels, where] = du.astype(BF16)
                field[2 * out_channels :, where] = shift_lanes(du, -1).astype(BF16)
            grad_ref[...] += lax.dot_general(
                field[...], patch[...], (((1,), (1,)), ((), ())), preferred_element_type=F32
            )

        return carry

    lax.fori_loop(0, slots, step, 0)


def spread_to_all(value, axis):
    count = lax.axis_size(axis)
    copies = jnp.broadcast_to(value[None], (count,) + value.shape)
    return lax.all_to_all(copies, axis, split_axis=0, concat_axis=0, tiled=True)


VM = pl.BlockSpec(memory_space=pltpu.VMEM)
SM = pl.BlockSpec(memory_space=pltpu.SMEM)


def call(kernel, dims, outs, ins, scratch, flops, args):
    return pl.pallas_call(
        functools.partial(kernel, dims),
        out_shape=outs,
        in_specs=ins,
        out_specs=jax.tree.map(lambda _: VM, outs),
        scratch_shapes=scratch,
        cost_estimate=pl.CostEstimate(flops=flops, bytes_accessed=1 << 22, transcendentals=0),
        compiler_params=pltpu.CompilerParams(vmem_limit_bytes=48 * 1024 * 1024),
    )(*args)


def per_device(features, labels, crop_block, weight, gain, shift, head, run_mean, run_var):
    slab = features[0]
    channels, planes, height, columns = slab.shape
    own_rows = weight.shape[0]
    devices = lax.axis_size("dev")
    own_index = lax.axis_index("dev")
    out_channels = own_rows * devices
    taps = 9 * channels
    blocks = height // CY
    cell_rows = planes * CY
    cells = cell_rows * columns
    table = crop_block[0]
    slots = table.shape[1]
    dims = (planes, blocks, channels, out_channels, columns, slots)

    weight_b = weight.astype(BF16).reshape(own_rows, 9, 3, channels).transpose(2, 0, 1, 3)
    vectors = jnp.stack([gain, shift, head, run_mean, run_var], 1).astype(BF16)
    vectors = jnp.pad(vectors, ((0, 0), (0, taps - vectors.shape[1])))
    own_params = jnp.concatenate([weight_b.reshape(3, own_rows, taps), vectors[None]], 0)
    params = spread_to_all(own_params, "dev").transpose(1, 0, 2, 3).reshape(4 * out_channels, taps)

    turned = jnp.pad(slab.transpose(1, 2, 0, 3), ((0, 0), (1, 1), (0, 0), (0, 0)))
    turned = turned.reshape(planes, (height + 2) * channels, columns)
    low = lax.ppermute(turned[planes - 1], "dev", [(i, i + 1) for i in range(devices - 1)])
    high = lax.ppermute(turned[0], "dev", [(i + 1, i) for i in range(devices - 1)])

    route = lax.dynamic_slice_in_dim(table, own_index, 1, 0)[0]
    live = (table >= 0).astype(F32)
    count = jnp.sum(live, 0) * cells
    counts = jnp.broadcast_to(count[:, None], (slots, LANES))
    live_wide = jnp.broadcast_to(live[:, :, None], live.shape + (LANES,))
    targets = labels[0].reshape(planes, blocks, CY, columns).transpose(1, 0, 2, 3)
    targets = targets.reshape(blocks, cell_rows, columns).astype(F32)

    shape = jax.ShapeDtypeStruct
    conv_flops = 2 * 27 * channels * out_channels * planes * height * columns
    patch = pltpu.VMEM((taps, cells), BF16)
    tile = pltpu.VMEM((LANES, LANES), F32)
    u, stats = call(
        forward_kernel,
        dims,
        (shape((blocks, out_channels, cells), BF16), shape((slots, LANES), F32)),
        [SM, VM, VM],
        [patch, tile, tile],
        conv_flops,
        (route, params, turned),
    )
    all_stats = spread_to_all(stats[None], "dev")
    all_stats = all_stats.reshape(devices, slots, LANES)
    scores = call(
        score_kernel,
        dims,
        shape((planes, height, columns), F32),
        [VM, VM, VM, VM],
        [pltpu.VMEM((taps, 8 * columns), BF16)],
        conv_flops,
        (params, turned, low, high),
    )
    sums, norms, vector_terms = call(
        sums_kernel,
        dims,
        (
            shape((slots, LANES), F32),
            shape((LANES, LANES), F32),
            shape((out_channels, columns), F32),
        ),
        [SM, SM, VM, VM, VM, VM, VM, VM],
        [tile, tile],
        conv_flops // 16,
        (route, count, params, u, targets, all_stats, live_wide, counts),
    )
    all_sums = spread_to_all(sums[None], "dev").reshape(devices, slots, LANES)
    terms = call(
        grad_kernel,
        dims,
        shape((3 * out_channels, taps), F32),
        [SM, SM, VM, VM, VM, VM, VM, VM, VM],
        [patch, pltpu.VMEM((3 * out_channels, cells), BF16), tile, tile],
        conv_flops,
        (route, count, params, turned, u, targets, all_sums, counts, norms),
    )
    terms = terms.reshape(3, devices, own_rows, taps).transpose(1, 0, 2, 3)
    vector_terms = jnp.pad(vector_terms, ((0, 0), (0, taps - columns)))
    vector_terms = vector_terms.reshape(devices, 1, own_rows, taps)
    packed = jnp.concatenate([terms, vector_terms], 1)
    packed = lax.all_to_all(packed, "dev", split_axis=0, concat_axis=0, tiled=True)
    part = jnp.sum(packed, 0)
    roles = lax.axis_size("role")
    total = part
    moving = part
    for _ in range(roles - 1):
        moving = lax.ppermute(moving, "role", [(i, (i + 1) % roles) for i in range(roles)])
        total = total + moving
    weight_grad = total[:3].reshape(3, own_rows, 9, channels).transpose(1, 2, 0, 3)
    return scores[None], weight_grad.reshape(own_rows, 27 * channels), total[3, :, :3]


def solution(mesh):
    in_specs = (
        P("role", None, "dev", None, None),
        P("role", "dev", None, None),
        P("role", None, None),
        P("dev", None),
        P("dev"),
        P("dev"),
        P("dev"),
        P("dev"),
        P("dev"),
    )
    out_specs = (P("role", "dev", None, None), P("dev", None), P("dev", None))
    return jax.shard_map(
        per_device, mesh=mesh, in_specs=in_specs, out_specs=out_specs, check_vma=False
    )
```

```python
import functools

import jax
import jax.numpy as jnp
from jax import lax
from jax.experimental import pallas as pl
from jax.experimental.pallas import tpu as pltpu
from jax.sharding import PartitionSpec as P

CY = 4
EPS = 1e-05
LANES = 128
F32 = jnp.float32
BF16 = jnp.bfloat16


def shift_lanes(value, offset):
    lane = lax.broadcasted_iota(jnp.int32, value.shape, 1)
    width = value.shape[1]
    if offset < 0:
        return jnp.where(lane == 0, 0.0, pltpu.roll(value, 1, 1))
    return jnp.where(lane == width - 1, 0.0, pltpu.roll(value, width - 1, 1))


def column(table, index):
    lane = lax.broadcasted_iota(jnp.int32, table.shape, 1)
    return jnp.sum(jnp.where(lane == index, table, 0.0), axis=1, keepdims=True)


def put_column(ref, rows, index, value):
    part = ref[rows, :]
    lane = lax.broadcasted_iota(jnp.int32, part.shape, 1)
    ref[rows, :] = jnp.where(lane == index, value, part)


def crop_tiles(planes, block, channels):
    for z in range(planes):
        for y in range(CY):
            cell_row = z * CY + y
            for dz in range(3):
                for dy in range(3):
                    zs, ys = z + dz - 1, y + dy - 1
                    if 0 <= zs < planes and 0 <= ys < CY:
                        yield (dz * 3 + dy) * channels, cell_row, zs, ys


def fill_patches(patch_ref, slab_ref, block, planes, channels, columns):
    base = pl.multiple_of((block * CY + 1) * channels, channels)
    for tap_row, cell_row, zs, ys in crop_tiles(planes, block, channels):
        patch_ref[pl.ds(tap_row, channels), pl.ds(cell_row * columns, columns)] = slab_ref[
            zs, pl.ds(base + ys * channels, channels), :
        ]


def conv_rows(weights, patch_ref, first, rows, out_channels, columns):
    taps = jnp.dot(
        weights,
        patch_ref[:, first * columns : (first + rows) * columns],
        preferred_element_type=F32,
    )
    results = []
    for row in range(rows):
        part = taps[:, row * columns : (row + 1) * columns]
        results.append(
            part[out_channels : 2 * out_channels]
            + shift_lanes(part[:out_channels], -1)
            + shift_lanes(part[2 * out_channels :], 1)
        )
    return results


def peer_of(me, step, count):
    return lax.rem(me + step, count)


def greet(axes):
    barrier = pltpu.get_barrier_semaphore()
    total = 0
    for axis, count in axes:
        me = lax.axis_index(axis)

        def tell(step, carry, axis=axis, count=count, me=me):
            pl.semaphore_signal(
                barrier,
                inc=1,
                device_id={axis: peer_of(me, step, count)},
                device_id_type=pl.DeviceIdType.MESH,
            )
            return carry

        lax.fori_loop(1, count, tell, 0)
        total += count - 1
    pl.semaphore_wait(barrier, total)


def to_peer(axis, count, step, source, target, sends, receives):
    me = lax.axis_index(axis)
    peer = peer_of(me, step, count)
    return pltpu.make_async_remote_copy(
        src_ref=source(peer),
        dst_ref=target.at[me],
        send_sem=sends.at[step],
        recv_sem=receives.at[step],
        device_id={axis: peer},
        device_id_type=pl.DeviceIdType.MESH,
    )


def start_all(*parts):
    def one(step, carry):
        to_peer(parts[0], parts[1], step, *parts[2:]).start()
        return carry

    lax.fori_loop(1, parts[1], one, 0)


def wait_all(*parts):
    def one(step, carry):
        to_peer(parts[0], parts[1], step, *parts[2:]).wait()
        return carry

    lax.fori_loop(1, parts[1], one, 0)


def one_hot(rows, columns, target):
    row = lax.broadcasted_iota(jnp.int32, (rows, columns), 0)
    return (lax.broadcasted_iota(jnp.int32, (rows, columns), 1) == target(row)).astype(F32)


def score_plane(dims, z, param_ref, slab_ref, low_ref, high_ref, out_ref, patch):
    planes, blocks, channels, out_channels, columns, slots = dims
    height = blocks * CY
    group = 8
    taps = 3 * channels
    vectors = param_ref[3 * out_channels :, :LANES].astype(F32)
    gain, shift, head, mean, spread = (vectors[:, k : k + 1] for k in range(5))
    inverse = lax.rsqrt(spread + EPS)

    def step(number, carry):
        for row in range(group):
            start = pl.multiple_of((number * group + row) * channels, channels)
            for dz in range(3):
                zs = z + dz - 1
                where = pl.ds(start, taps)
                if zs < 0:
                    piece = low_ref[where, :]
                elif zs >= planes:
                    piece = high_ref[where, :]
                else:
                    piece = slab_ref[zs, where, :]
                patch[dz * taps : (dz + 1) * taps, row * columns : (row + 1) * columns] = piece
        weights = param_ref[0 : 3 * out_channels, :]
        lines = []
        for first in range(0, group, 2):
            for value in conv_rows(weights, patch, first, 2, out_channels, columns):
                hidden = jnp.maximum(gain * ((value - mean) * inverse) + shift, 0.0)
                lines.append(jnp.sum(head * hidden, axis=0, keepdims=True))
        out_ref[pl.ds(pl.multiple_of(number * group, group), group), :] = jnp.concatenate(
            lines, axis=0
        )
        return carry

    lax.fori_loop(0, height // group, step, 0)


def forward_kernel(
    dims,
    count,
    own_rows,
    route_ref,
    gain_ref,
    shift_ref,
    head_ref,
    mean_ref,
    spread_ref,
    weight_ref,
    slab_ref,
    live_ref,
    counts_ref,
    param_ref,
    u_ref,
    norm_ref,
    high_out,
    score_ref,
    patch,
    table,
    turned,
    own,
    held,
    stat,
    stats,
    low,
    high,
    sends,
    receives,
    stat_sends,
    stat_receives,
    halo_sends,
    halo_receives,
):
    planes, blocks, channels, out_channels, columns, slots = dims
    cell_rows = planes * CY
    cells = cell_rows * columns
    me = lax.axis_index("dev")
    rows = own.shape[0]
    tile = weight_ref[...]
    row = lax.broadcasted_iota(jnp.int32, tile.shape, 0)
    lane = lax.broadcasted_iota(jnp.int32, tile.shape, 1)
    for k, ref in enumerate((gain_ref, shift_ref, head_ref, mean_ref, spread_ref)):
        for o in range(own_rows):
            tile = jnp.where((row == 3 * own_rows + o) & (lane == k), ref[o], tile)
    own[...] = tile.astype(BF16)
    greet((("dev", count),))
    exchange = ("dev", count, lambda peer: own, held, sends, receives)
    start_all(*exchange)

    def halo(way):
        return pltpu.make_async_remote_copy(
            src_ref=slab_ref.at[planes - 1 if way == 0 else 0],
            dst_ref=low if way == 0 else high,
            send_sem=halo_sends.at[way],
            recv_sem=halo_receives.at[way],
            device_id={"dev": lax.rem(me + (1 if way == 0 else count - 1), count)},
            device_id_type=pl.DeviceIdType.MESH,
        )

    @pl.when(me < count - 1)
    def _():
        halo(0).start()

    @pl.when(me > 0)
    def _():
        halo(1).start()

    @pl.when(me == 0)
    def _():
        low[...] = jnp.zeros_like(low)

    @pl.when(me == count - 1)
    def _():
        high[...] = jnp.zeros_like(high)

    held[me] = own[...]
    patch[...] = jnp.zeros_like(patch)
    table[...] = jnp.zeros_like(table)
    order = one_hot(
        4 * out_channels,
        count * rows,
        lambda r: (r % out_channels) // own_rows * rows
        + r // out_channels * own_rows
        + r % own_rows,
    ).astype(BF16)
    wait_all(*exchange)
    param_ref[...] = jnp.dot(
        order, held[...].reshape(count * rows, -1), preferred_element_type=F32
    ).astype(BF16)

    def step(block, carry):
        fill_patches(patch, slab_ref, block, planes, channels, columns)
        weights = param_ref[0 : 3 * out_channels, :]
        total = jnp.zeros((out_channels, columns), F32)
        for first in range(0, cell_rows, 2):
            lines = conv_rows(weights, patch, first, 2, out_channels, columns)
            for k, line in enumerate(lines):
                rounded = line.astype(BF16)
                u_ref[block, :, (first + k) * columns : (first + k + 1) * columns] = rounded
                total = total + rounded.astype(F32)
        total = jnp.sum(total, axis=1, keepdims=True)
        mean = total * (1.0 / cells)
        square = jnp.zeros((out_channels, columns), F32)
        for r in range(cell_rows):
            diff = u_ref[block, :, r * columns : (r + 1) * columns].astype(F32) - mean
            square = square + diff * diff
        square = jnp.sum(square, axis=1, keepdims=True)
        put_column(table, slice(0, out_channels), block, total)
        put_column(table, slice(out_channels, 2 * out_channels), block, square)
        return carry

    lax.fori_loop(0, blocks, step, 0)
    turned[...] = jnp.transpose(table[...])

    def route(slot, carry):
        block = route_ref[slot]
        entry = turned[pl.ds(jnp.maximum(block, 0), 1), :]
        stat[pl.ds(slot, 1), :] = jnp.where(block >= 0, entry, 0.0)
        return carry

    lax.fori_loop(0, slots, route, 0)
    exchange = ("dev", count, lambda peer: stat, stats, stat_sends, stat_receives)
    start_all(*exchange)
    stats[me] = stat[...]

    @pl.when(me < count - 1)
    def _():
        halo(0).wait_send()
        halo(1).wait_recv()

    @pl.when(me > 0)
    def _():
        halo(1).wait_send()
        halo(0).wait_recv()

    high_out[...] = high[...]
    score_plane(dims, 0, param_ref, slab_ref, low, high, score_ref.at[0], patch)
    for z in range(1, planes - 1):
        score_plane(dims, z, param_ref, slab_ref, low, high, score_ref.at[z], patch)
    wait_all(*exchange)

    total = stats[0]
    for s in range(1, count):
        total = total + stats[s]
    counts = counts_ref[...]
    mu = total / counts
    spread = jnp.zeros_like(mu)
    for s in range(count):
        entry = stats[s]
        diff = entry * (1.0 / cells) - mu
        spread = spread + (
            pltpu.roll(entry, LANES - out_channels, 1) + live_ref[s] * cells * (diff * diff)
        )
    inverse = lax.rsqrt(spread / counts + EPS)
    wide = lax.broadcasted_iota(jnp.int32, mu.shape, 1)
    table[...] = jnp.zeros_like(table)
    table[0:slots, :] = jnp.where(wide < out_channels, mu, pltpu.roll(inverse, out_channels, 1))
    norm_ref[...] = jnp.transpose(table[...])


def means_kernel(
    dims,
    count,
    param_ref,
    slab_ref,
    high_ref,
    sum_ref,
    counts_ref,
    mean_ref,
    score_ref,
    patch,
    table,
    held,
    sends,
    receives,
):
    planes, slots = dims[0], dims[5]
    greet((("dev", count),))
    exchange = ("dev", count, lambda peer: sum_ref, held, sends, receives)
    start_all(*exchange)
    held[lax.axis_index("dev")] = sum_ref[...]
    score_plane(dims, planes - 1, param_ref, slab_ref, high_ref, high_ref, score_ref, patch)
    wait_all(*exchange)
    total = held[0]
    for s in range(1, count):
        total = total + held[s]
    table[...] = jnp.zeros_like(table)
    table[0:slots, :] = total / counts_ref[...]
    mean_ref[...] = jnp.transpose(table[...])


def scatter_kernel(
    count, roles, chunk_ref, out_ref, held, part, others, sends, receives, role_sends, role_receives
):
    me = lax.axis_index("dev")
    greet((("dev", count), ("role", roles)))
    exchange = ("dev", count, lambda peer: chunk_ref.at[peer], held, sends, receives)
    start_all(*exchange)
    held[me] = chunk_ref[me]
    wait_all(*exchange)
    total = held[0]
    for s in range(1, count):
        total = total + held[s]
    part[...] = total
    exchange = ("role", roles, lambda peer: part, others, role_sends, role_receives)
    start_all(*exchange)
    others[lax.axis_index("role")] = total
    wait_all(*exchange)
    total = others[0]
    for r in range(1, roles):
        total = total + others[r]
    out_ref[...] = total


def crop_row(u_ref, label_ref, block, row, columns, mu, inverse, vectors, count):
    gain, shift, head = vectors
    value = u_ref[block, :, row * columns : (row + 1) * columns].astype(F32)
    normal = (value - mu) * inverse
    before = gain * normal + shift
    hidden = jnp.maximum(before, 0.0)
    score = jnp.sum(head * hidden, axis=0, keepdims=True)
    residual = (score - label_ref[block, row : row + 1, :]) / count
    dbefore = jnp.where(before > 0, head * residual, 0.0)
    return normal, hidden, residual, dbefore


def sums_kernel(
    dims,
    route_ref,
    count_ref,
    param_ref,
    u_ref,
    label_ref,
    norm_ref,
    sum_ref,
    vec_ref,
    square,
    table,
):
    planes, blocks, channels, out_channels, columns, slots = dims
    cell_rows = planes * CY
    table[...] = jnp.zeros_like(table)
    vec_ref[...] = jnp.zeros_like(vec_ref)

    def step(slot, carry):
        block = route_ref[slot]

        @pl.when(block >= 0)
        def _():
            vec = param_ref[3 * out_channels :, :LANES].astype(F32)
            vectors = tuple(vec[:, k : k + 1] for k in range(3))
            pair = column(norm_ref[...], slot)
            mean, inv = pair[:out_channels], pair[out_channels:]
            cell_count = count_ref[slot]
            first = jnp.zeros((out_channels, columns), F32)
            second, third = first, first
            for row in range(cell_rows):
                normal, hidden, residual, dbefore = crop_row(
                    u_ref, label_ref, block, row, columns, mean, inv, vectors, cell_count
                )
                first = first + dbefore
                second = second + dbefore * normal
                third = third + hidden * residual
            put_column(
                table, slice(0, out_channels), slot, jnp.sum(first, axis=1, keepdims=True)
            )
            put_column(
                table,
                slice(out_channels, 2 * out_channels),
                slot,
                jnp.sum(second, axis=1, keepdims=True),
            )
            vec_ref[...] += third

        return carry

    lax.fori_loop(0, slots, step, 0)
    both = table[...]
    sums = jnp.sum(both, axis=1, keepdims=True)
    last = jnp.sum(vec_ref[...], axis=1, keepdims=True)
    wide = lax.broadcasted_iota(jnp.int32, vec_ref.shape, 1)
    vec_ref[...] = jnp.where(
        wide == 0,
        sums[out_channels:],
        jnp.where(wide == 1, sums[:out_channels], jnp.where(wide == 2, last, 0.0)),
    )
    square[...] = jnp.transpose(both)
    sum_ref[...] = square[0:slots, :]


def grad_kernel(
    dims,
    route_ref,
    count_ref,
    param_ref,
    slab_ref,
    u_ref,
    label_ref,
    norm_ref,
    means,
    vec_ref,
    pack_ref,
    patch,
    field,
    grad_ref,
):
    planes, blocks, channels, out_channels, columns, slots = dims
    cell_rows = planes * CY
    count, rows, taps = pack_ref.shape
    own_rows = out_channels // count
    patch[...] = jnp.zeros_like(patch)
    grad_ref[...] = jnp.zeros_like(grad_ref)

    def step(slot, carry):
        block = route_ref[slot]

        @pl.when(block >= 0)
        def _():
            vec = param_ref[3 * out_channels :, :LANES].astype(F32)
            vectors = tuple(vec[:, k : k + 1] for k in range(3))
            gain = vectors[0]
            pair = column(norm_ref[...], slot)
            mean, inv = pair[:out_channels], pair[out_channels:]
            pair = column(means[...], slot)
            first, second = gain * pair[:out_channels], gain * pair[out_channels:]
            cell_count = count_ref[slot]
            fill_patches(patch, slab_ref, block, planes, channels, columns)
            for row in range(cell_rows):
                normal, hidden, residual, dbefore = crop_row(
                    u_ref, label_ref, block, row, columns, mean, inv, vectors, cell_count
                )
                du = inv * (dbefore * gain - first - normal * second)
                du = du.astype(BF16).astype(F32)
                where = slice(row * columns, (row + 1) * columns)
                field[0:out_channels, where] = shift_lanes(du, 1).astype(BF16)
                field[out_channels : 2 * out_channels, where] = du.astype(BF16)
                field[2 * out_channels :, where] = shift_lanes(du, -1).astype(BF16)
            grad_ref[0 : 3 * out_channels, :] += lax.dot_general(
                field[...], patch[...], (((1,), (1,)), ((), ())), preferred_element_type=F32
            )

        return carry

    lax.fori_loop(0, slots, step, 0)
    grad_ref[3 * out_channels :, 0:LANES] = vec_ref[...]
    order = one_hot(
        count * rows,
        4 * out_channels,
        lambda r: jnp.where(
            r % rows < 4 * own_rows,
            r % rows // own_rows * out_channels + r // rows * own_rows + r % own_rows,
            -1,
        ),
    )
    packed = jnp.dot(
        order, grad_ref[...], precision=lax.Precision.HIGHEST, preferred_element_type=F32
    )
    pack_ref[...] = packed.reshape(count, rows, taps)


VM = pl.BlockSpec(memory_space=pltpu.VMEM)
SM = pl.BlockSpec(memory_space=pltpu.SMEM)


def call(kernel, outs, ins, scratch, flops, args, collective=None):
    extra = {} if collective is None else {"collective_id": collective, "has_side_effects": True}
    return pl.pallas_call(
        kernel,
        out_shape=outs,
        in_specs=ins,
        out_specs=jax.tree.map(lambda _: VM, outs),
        scratch_shapes=scratch,
        cost_estimate=pl.CostEstimate(flops=flops, bytes_accessed=1 << 22, transcendentals=0),
        compiler_params=pltpu.CompilerParams(vmem_limit_bytes=48 * 1024 * 1024, **extra),
    )(*args)


def per_device(features, labels, crop_block, weight, gain, shift, head, run_mean, run_var):
    slab = features[0]
    channels, planes, height, columns = slab.shape
    own_rows = weight.shape[0]
    devices = lax.axis_size("dev")
    roles = lax.axis_size("role")
    own_index = lax.axis_index("dev")
    out_channels = own_rows * devices
    taps = 9 * channels
    blocks = height // CY
    cell_rows = planes * CY
    cells = cell_rows * columns
    table = crop_block[0]
    slots = table.shape[1]
    dims = (planes, blocks, channels, out_channels, columns, slots)
    rows = -(-4 * own_rows // 16) * 16

    own_weight = weight.reshape(own_rows, 9, 3, channels).transpose(2, 0, 1, 3)
    own_weight = own_weight.reshape(3 * own_rows, taps)
    own_weight = jnp.pad(own_weight, ((0, rows - 3 * own_rows), (0, 0)))
    turned = jnp.pad(slab.transpose(1, 2, 0, 3), ((0, 0), (1, 1), (0, 0), (0, 0)))
    turned = turned.reshape(planes, (height + 2) * channels, columns)
    route = lax.dynamic_slice_in_dim(table, own_index, 1, 0)[0]
    live = (table >= 0).astype(F32)
    count = jnp.sum(live, 0) * cells
    counts = jnp.broadcast_to(count[:, None], (slots, LANES))
    live_wide = jnp.broadcast_to(live[:, :, None], live.shape + (LANES,))
    targets = labels[0].reshape(planes, blocks, CY, columns).transpose(1, 0, 2, 3)
    targets = targets.reshape(blocks, cell_rows, columns).astype(F32)

    shape = jax.ShapeDtypeStruct
    conv_flops = 2 * 27 * channels * out_channels * planes * height * columns
    patch = pltpu.VMEM((taps, cells), BF16)
    score_patch = pltpu.VMEM((taps, 8 * columns), BF16)
    tile = pltpu.VMEM((LANES, LANES), F32)
    small = pltpu.VMEM((slots, LANES), F32)
    held = pltpu.VMEM((devices, slots, LANES), F32)
    plane = pltpu.VMEM(turned.shape[1:], BF16)
    signals = pltpu.SemaphoreType.DMA((devices,))
    pair = pltpu.SemaphoreType.DMA((2,))
    params, u, norms, high, scores = call(
        functools.partial(forward_kernel, dims, devices, own_rows),
        (
            shape((4 * out_channels, taps), BF16),
            shape((blocks, out_channels, cells), BF16),
            shape((LANES, LANES), F32),
            shape(turned.shape[1:], BF16),
            shape((planes - 1, height, columns), F32),
        ),
        [SM] * 6 + [VM] * 4,
        [patch, tile, tile, pltpu.VMEM((rows, taps), BF16)]
        + [pltpu.VMEM((devices, rows, taps), BF16), small, held, plane, plane]
        + [signals] * 4
        + [pair] * 2,
        conv_flops * 2,
        (route, gain, shift, head, run_mean, run_var, own_weight, turned, live_wide, counts),
        0,
    )
    sums, vector_terms = call(
        functools.partial(sums_kernel, dims),
        (shape((slots, LANES), F32), shape((out_channels, columns), F32)),
        [SM, SM, VM, VM, VM, VM],
        [tile, tile],
        conv_flops // 16,
        (route, count, params, u, targets, norms),
    )
    means, last_scores = call(
        functools.partial(means_kernel, dims, devices),
        (shape((LANES, LANES), F32), shape((height, columns), F32)),
        [VM] * 5,
        [score_patch, tile, held, signals, signals],
        conv_flops,
        (params, turned, high, sums, counts),
        1,
    )
    packed = call(
        functools.partial(grad_kernel, dims),
        shape((devices, rows, taps), F32),
        [SM, SM] + [VM] * 7,
        [patch, pltpu.VMEM((3 * out_channels, cells), BF16)]
        + [pltpu.VMEM((4 * out_channels, taps), F32)],
        conv_flops,
        (route, count, params, turned, u, targets, norms, means, vector_terms),
    )
    part = pltpu.VMEM((rows, taps), F32)
    role_signals = pltpu.SemaphoreType.DMA((roles,))
    total = call(
        functools.partial(scatter_kernel, devices, roles),
        shape((rows, taps), F32),
        [VM],
        [pltpu.VMEM((devices, rows, taps), F32), part, pltpu.VMEM((roles, rows, taps), F32)]
        + [signals, signals, role_signals, role_signals],
        conv_flops // 16,
        (packed,),
        2,
    )
    weight_grad = total[: 3 * own_rows].reshape(3, own_rows, 9, channels).transpose(1, 2, 0, 3)
    weight_grad = weight_grad.reshape(own_rows, 27 * channels)
    vector_grad = total[3 * own_rows : 4 * own_rows, :3]
    return jnp.concatenate([scores, last_scores[None]], 0)[None], weight_grad, vector_grad


def solution(mesh):
    in_specs = (
        P("role", None, "dev", None, None),
        P("role", "dev", None, None),
        P("role", None, None),
        P("dev", None),
        P("dev"),
        P("dev"),
        P("dev"),
        P("dev"),
        P("dev"),
    )
    out_specs = (P("role", "dev", None, None), P("dev", None), P("dev", None))
    return jax.shard_map(
        per_device, mesh=mesh, in_specs=in_specs, out_specs=out_specs, check_vma=False
    )
```

```python
import functools

import jax
import jax.numpy as jnp
from jax import lax
from jax.experimental import pallas as pl
from jax.experimental.pallas import tpu as pltpu
from jax.sharding import PartitionSpec as P

CY = 4
EPS = 1e-05
LANES = 128
F32 = jnp.float32
BF16 = jnp.bfloat16


def shift_lanes(value, offset):
    lane = lax.broadcasted_iota(jnp.int32, value.shape, 1)
    width = value.shape[1]
    if offset < 0:
        return jnp.where(lane == 0, 0.0, pltpu.roll(value, 1, 1))
    return jnp.where(lane == width - 1, 0.0, pltpu.roll(value, width - 1, 1))


def column(table, index):
    lane = lax.broadcasted_iota(jnp.int32, table.shape, 1)
    return jnp.sum(jnp.where(lane == index, table, 0.0), axis=1, keepdims=True)


def put_column(ref, rows, index, value):
    part = ref[rows, :]
    lane = lax.broadcasted_iota(jnp.int32, part.shape, 1)
    ref[rows, :] = jnp.where(lane == index, value, part)


def crop_tiles(planes, block, channels):
    for z in range(planes):
        for y in range(CY):
            cell_row = z * CY + y
            for dz in range(3):
                for dy in range(3):
                    zs, ys = z + dz - 1, y + dy - 1
                    if 0 <= zs < planes and 0 <= ys < CY:
                        yield (dz * 3 + dy) * channels, cell_row, zs, ys


def fill_patches(patch_ref, slab_ref, block, planes, channels, columns):
    base = pl.multiple_of((block * CY + 1) * channels, channels)
    for tap_row, cell_row, zs, ys in crop_tiles(planes, block, channels):
        patch_ref[pl.ds(tap_row, channels), pl.ds(cell_row * columns, columns)] = slab_ref[
            zs, pl.ds(base + ys * channels, channels), :
        ]


def conv_rows(weights, patch_ref, first, rows, out_channels, columns):
    taps = jnp.dot(
        weights,
        patch_ref[:, first * columns : (first + rows) * columns],
        preferred_element_type=F32,
    )
    results = []
    for row in range(rows):
        part = taps[:, row * columns : (row + 1) * columns]
        results.append(
            part[out_channels : 2 * out_channels]
            + shift_lanes(part[:out_channels], -1)
            + shift_lanes(part[2 * out_channels :], 1)
        )
    return results


def peer_of(me, step, count):
    return lax.rem(me + step, count)


def greet(axes):
    barrier = pltpu.get_barrier_semaphore()
    total = 0
    for axis, count in axes:
        me = lax.axis_index(axis)

        def tell(step, carry, axis=axis, count=count, me=me):
            pl.semaphore_signal(
                barrier,
                inc=1,
                device_id={axis: peer_of(me, step, count)},
                device_id_type=pl.DeviceIdType.MESH,
            )
            return carry

        lax.fori_loop(1, count, tell, 0)
        total += count - 1
    pl.semaphore_wait(barrier, total)


def to_peer(axis, count, step, source, target, sends, receives):
    me = lax.axis_index(axis)
    peer = peer_of(me, step, count)
    return pltpu.make_async_remote_copy(
        src_ref=source(peer),
        dst_ref=target.at[me],
        send_sem=sends.at[step],
        recv_sem=receives.at[step],
        device_id={axis: peer},
        device_id_type=pl.DeviceIdType.MESH,
    )


def start_all(*parts):
    def one(step, carry):
        to_peer(parts[0], parts[1], step, *parts[2:]).start()
        return carry

    lax.fori_loop(1, parts[1], one, 0)


def wait_all(*parts):
    def one(step, carry):
        to_peer(parts[0], parts[1], step, *parts[2:]).wait()
        return carry

    lax.fori_loop(1, parts[1], one, 0)


def one_hot(rows, columns, target):
    row = lax.broadcasted_iota(jnp.int32, (rows, 1), 0)
    return (lax.broadcasted_iota(jnp.int32, (rows, columns), 1) == target(row)).astype(F32)


def score_plane(dims, z, param_ref, slab_ref, low_ref, high_ref, out_ref, patch):
    planes, blocks, channels, out_channels, columns, slots = dims
    height = blocks * CY
    group = 8
    taps = 3 * channels
    vectors = param_ref[3 * out_channels :, :LANES].astype(F32)
    gain, shift, head, mean, spread = (vectors[:, k : k + 1] for k in range(5))
    inverse = lax.rsqrt(spread + EPS)

    def step(number, carry):
        for row in range(group):
            start = pl.multiple_of((number * group + row) * channels, channels)
            for dz in range(3):
                zs = z + dz - 1
                where = pl.ds(start, taps)
                if zs < 0:
                    piece = low_ref[where, :]
                elif zs >= planes:
                    piece = high_ref[where, :]
                else:
                    piece = slab_ref[zs, where, :]
                patch[dz * taps : (dz + 1) * taps, row * columns : (row + 1) * columns] = piece
        weights = param_ref[0 : 3 * out_channels, :]
        lines = []
        for first in range(0, group, 2):
            for value in conv_rows(weights, patch, first, 2, out_channels, columns):
                hidden = jnp.maximum(gain * ((value - mean) * inverse) + shift, 0.0)
                lines.append(jnp.sum(head * hidden, axis=0, keepdims=True))
        out_ref[pl.ds(pl.multiple_of(number * group, group), group), :] = jnp.concatenate(
            lines, axis=0
        )
        return carry

    lax.fori_loop(0, height // group, step, 0)


def forward_kernel(
    dims,
    count,
    own_rows,
    route_ref,
    gain_ref,
    shift_ref,
    head_ref,
    mean_ref,
    spread_ref,
    weight_ref,
    slab_ref,
    live_ref,
    counts_ref,
    param_ref,
    u_ref,
    norm_ref,
    high_out,
    score_ref,
    patch,
    table,
    turned,
    own,
    held,
    stat,
    stats,
    low,
    high,
    sends,
    receives,
    stat_sends,
    stat_receives,
    halo_sends,
    halo_receives,
):
    planes, blocks, channels, out_channels, columns, slots = dims
    cell_rows = planes * CY
    cells = cell_rows * columns
    me = lax.axis_index("dev")
    rows = own.shape[0]
    tile = weight_ref[...]
    row = lax.broadcasted_iota(jnp.int32, tile.shape, 0)
    lane = lax.broadcasted_iota(jnp.int32, tile.shape, 1)
    for k, ref in enumerate((gain_ref, shift_ref, head_ref, mean_ref, spread_ref)):
        for o in range(own_rows):
            tile = jnp.where((row == 3 * own_rows + o) & (lane == k), ref[o], tile)
    own[...] = tile.astype(BF16)
    greet((("dev", count),))
    exchange = ("dev", count, lambda peer: own, held, sends, receives)
    start_all(*exchange)

    def halo(way):
        return pltpu.make_async_remote_copy(
            src_ref=slab_ref.at[planes - 1 if way == 0 else 0],
            dst_ref=low if way == 0 else high,
            send_sem=halo_sends.at[way],
            recv_sem=halo_receives.at[way],
            device_id={"dev": lax.rem(me + (1 if way == 0 else count - 1), count)},
            device_id_type=pl.DeviceIdType.MESH,
        )

    @pl.when(me == 0)
    def _():
        low[...] = jnp.zeros_like(low)

    @pl.when(me == count - 1)
    def _():
        high[...] = jnp.zeros_like(high)

    held[me] = own[...]
    patch[...] = jnp.zeros_like(patch)
    table[...] = jnp.zeros_like(table)
    order = one_hot(
        4 * out_channels,
        count * rows,
        lambda r: (r % out_channels) // own_rows * rows
        + r // out_channels * own_rows
        + r % own_rows,
    ).astype(BF16)
    wait_all(*exchange)

    @pl.when(me < count - 1)
    def _():
        halo(0).start()

    @pl.when(me > 0)
    def _():
        halo(1).start()

    param_ref[...] = jnp.dot(
        order, held[...].reshape(count * rows, -1), preferred_element_type=F32
    ).astype(BF16)

    def step(block, carry):
        fill_patches(patch, slab_ref, block, planes, channels, columns)
        weights = param_ref[0 : 3 * out_channels, :]
        total = jnp.zeros((out_channels, columns), F32)
        for first in range(0, cell_rows, 2):
            lines = conv_rows(weights, patch, first, 2, out_channels, columns)
            for k, line in enumerate(lines):
                rounded = line.astype(BF16)
                u_ref[block, :, (first + k) * columns : (first + k + 1) * columns] = rounded
                total = total + rounded.astype(F32)
        total = jnp.sum(total, axis=1, keepdims=True)
        mean = total * (1.0 / cells)
        square = jnp.zeros((out_channels, columns), F32)
        for r in range(cell_rows):
            diff = u_ref[block, :, r * columns : (r + 1) * columns].astype(F32) - mean
            square = square + diff * diff
        square = jnp.sum(square, axis=1, keepdims=True)
        put_column(table, slice(0, out_channels), block, total)
        put_column(table, slice(out_channels, 2 * out_channels), block, square)
        return carry

    lax.fori_loop(0, blocks, step, 0)
    turned[...] = jnp.transpose(table[...])

    def route(slot, carry):
        block = route_ref[slot]
        entry = turned[pl.ds(jnp.maximum(block, 0), 1), :]
        stat[pl.ds(slot, 1), :] = jnp.where(block >= 0, entry, 0.0)
        return carry

    lax.fori_loop(0, slots, route, 0)
    exchange = ("dev", count, lambda peer: stat, stats, stat_sends, stat_receives)
    start_all(*exchange)
    stats[me] = stat[...]

    @pl.when(me < count - 1)
    def _():
        halo(0).wait_send()
        halo(1).wait_recv()

    @pl.when(me > 0)
    def _():
        halo(1).wait_send()
        halo(0).wait_recv()

    high_out[...] = high[...]
    score_plane(dims, 0, param_ref, slab_ref, low, high, score_ref.at[0], patch)
    for z in range(1, planes - 1):
        score_plane(dims, z, param_ref, slab_ref, low, high, score_ref.at[z], patch)
    wait_all(*exchange)

    total = stats[0]
    for s in range(1, count):
        total = total + stats[s]
    counts = counts_ref[...]
    mu = total / counts
    spread = jnp.zeros_like(mu)
    for s in range(count):
        entry = stats[s]
        diff = entry * (1.0 / cells) - mu
        spread = spread + (
            pltpu.roll(entry, LANES - out_channels, 1) + live_ref[s] * cells * (diff * diff)
        )
    inverse = lax.rsqrt(spread / counts + EPS)
    wide = lax.broadcasted_iota(jnp.int32, mu.shape, 1)
    table[...] = jnp.zeros_like(table)
    table[0:slots, :] = jnp.where(wide < out_channels, mu, pltpu.roll(inverse, out_channels, 1))
    norm_ref[...] = jnp.transpose(table[...])


def means_kernel(
    dims,
    count,
    param_ref,
    slab_ref,
    high_ref,
    sum_ref,
    counts_ref,
    mean_ref,
    score_ref,
    patch,
    table,
    held,
    sends,
    receives,
):
    planes, slots = dims[0], dims[5]
    greet((("dev", count),))
    exchange = ("dev", count, lambda peer: sum_ref, held, sends, receives)
    start_all(*exchange)
    held[lax.axis_index("dev")] = sum_ref[...]
    score_plane(dims, planes - 1, param_ref, slab_ref, high_ref, high_ref, score_ref, patch)
    wait_all(*exchange)
    total = held[0]
    for s in range(1, count):
        total = total + held[s]
    table[...] = jnp.zeros_like(table)
    table[0:slots, :] = total / counts_ref[...]
    mean_ref[...] = jnp.transpose(table[...])


def scatter_kernel(
    count,
    roles,
    chunk_ref,
    out_ref,
    near,
    mine,
    held,
    part,
    others,
    pair_sends,
    pair_receives,
    sends,
    receives,
    role_sends,
    role_receives,
):
    me = lax.axis_index("dev")
    side, chip, chips = lax.rem(me, 2), lax.div(me, 2), count // 2
    greet((("dev", count), ("role", roles)))
    swap = pltpu.make_async_remote_copy(
        src_ref=chunk_ref.at[1 - side],
        dst_ref=near,
        send_sem=pair_sends.at[0],
        recv_sem=pair_receives.at[0],
        device_id={"dev": me + 1 - 2 * side},
        device_id_type=pl.DeviceIdType.MESH,
    )
    swap.start()
    swap.wait()
    mine[...] = chunk_ref[side] + near[...]

    def to_chip(step):
        peer = lax.rem(chip + step, chips)
        return pltpu.make_async_remote_copy(
            src_ref=mine.at[peer],
            dst_ref=held.at[chip],
            send_sem=sends.at[step],
            recv_sem=receives.at[step],
            device_id={"dev": peer * 2 + side},
            device_id_type=pl.DeviceIdType.MESH,
        )

    def start(step, carry):
        to_chip(step).start()
        return carry

    def wait(step, carry):
        to_chip(step).wait()
        return carry

    lax.fori_loop(1, chips, start, 0)
    held[chip] = mine[chip]
    lax.fori_loop(1, chips, wait, 0)
    total = held[0]
    for s in range(1, chips):
        total = total + held[s]
    part[...] = total
    exchange = ("role", roles, lambda peer: part, others, role_sends, role_receives)
    start_all(*exchange)
    others[lax.axis_index("role")] = total
    wait_all(*exchange)
    total = others[0]
    for r in range(1, roles):
        total = total + others[r]
    out_ref[...] = total


def crop_row(u_ref, label_ref, block, row, columns, mu, inverse, vectors, count):
    gain, shift, head = vectors
    value = u_ref[block, :, row * columns : (row + 1) * columns].astype(F32)
    normal = (value - mu) * inverse
    before = gain * normal + shift
    hidden = jnp.maximum(before, 0.0)
    score = jnp.sum(head * hidden, axis=0, keepdims=True)
    residual = (score - label_ref[block, row : row + 1, :]) / count
    dbefore = jnp.where(before > 0, head * residual, 0.0)
    return normal, hidden, residual, dbefore


def sums_kernel(
    dims,
    route_ref,
    count_ref,
    param_ref,
    u_ref,
    label_ref,
    norm_ref,
    sum_ref,
    vec_ref,
    square,
    table,
):
    planes, blocks, channels, out_channels, columns, slots = dims
    cell_rows = planes * CY
    table[...] = jnp.zeros_like(table)
    vec_ref[...] = jnp.zeros_like(vec_ref)

    def step(slot, carry):
        block = route_ref[slot]

        @pl.when(block >= 0)
        def _():
            vec = param_ref[3 * out_channels :, :LANES].astype(F32)
            vectors = tuple(vec[:, k : k + 1] for k in range(3))
            pair = column(norm_ref[...], slot)
            mean, inv = pair[:out_channels], pair[out_channels:]
            cell_count = count_ref[slot]
            first = jnp.zeros((out_channels, columns), F32)
            second, third = first, first
            for row in range(cell_rows):
                normal, hidden, residual, dbefore = crop_row(
                    u_ref, label_ref, block, row, columns, mean, inv, vectors, cell_count
                )
                first = first + dbefore
                second = second + dbefore * normal
                third = third + hidden * residual
            put_column(
                table, slice(0, out_channels), slot, jnp.sum(first, axis=1, keepdims=True)
            )
            put_column(
                table,
                slice(out_channels, 2 * out_channels),
                slot,
                jnp.sum(second, axis=1, keepdims=True),
            )
            vec_ref[...] += third

        return carry

    lax.fori_loop(0, slots, step, 0)
    both = table[...]
    sums = jnp.sum(both, axis=1, keepdims=True)
    last = jnp.sum(vec_ref[...], axis=1, keepdims=True)
    wide = lax.broadcasted_iota(jnp.int32, vec_ref.shape, 1)
    vec_ref[...] = jnp.where(
        wide == 0,
        sums[out_channels:],
        jnp.where(wide == 1, sums[:out_channels], jnp.where(wide == 2, last, 0.0)),
    )
    square[...] = jnp.transpose(both)
    sum_ref[...] = square[0:slots, :]


def grad_kernel(
    dims,
    route_ref,
    count_ref,
    param_ref,
    slab_ref,
    u_ref,
    label_ref,
    norm_ref,
    means,
    vec_ref,
    pack_ref,
    patch,
    field,
    grad_ref,
    tail_ref,
):
    planes, blocks, channels, out_channels, columns, slots = dims
    cell_rows = planes * CY
    count = 2 * pack_ref.shape[1]
    own_rows = out_channels // count
    taps = 9 * channels
    patch[...] = jnp.zeros_like(patch)
    grad_ref[...] = jnp.zeros_like(grad_ref)

    def step(slot, carry):
        block = route_ref[slot]

        @pl.when(block >= 0)
        def _():
            vec = param_ref[3 * out_channels :, :LANES].astype(F32)
            vectors = tuple(vec[:, k : k + 1] for k in range(3))
            gain = vectors[0]
            pair = column(norm_ref[...], slot)
            mean, inv = pair[:out_channels], pair[out_channels:]
            pair = column(means[...], slot)
            first, second = gain * pair[:out_channels], gain * pair[out_channels:]
            cell_count = count_ref[slot]
            fill_patches(patch, slab_ref, block, planes, channels, columns)
            for row in range(cell_rows):
                normal, hidden, residual, dbefore = crop_row(
                    u_ref, label_ref, block, row, columns, mean, inv, vectors, cell_count
                )
                du = inv * (dbefore * gain - first - normal * second)
                du = du.astype(BF16).astype(F32)
                where = slice(row * columns, (row + 1) * columns)
                field[0:out_channels, where] = shift_lanes(du, 1).astype(BF16)
                field[out_channels : 2 * out_channels, where] = du.astype(BF16)
                field[2 * out_channels :, where] = shift_lanes(du, -1).astype(BF16)
            grad_ref[:, 0:taps] += lax.dot_general(
                field[...], patch[...], (((1,), (1,)), ((), ())), preferred_element_type=F32
            )

        return carry

    lax.fori_loop(0, slots, step, 0)
    full = taps // LANES
    rest = taps - full * LANES
    tail = pltpu.roll(vec_ref[...], 3 * rest, 1)
    for tap in range(3):
        part = grad_ref[tap * out_channels : (tap + 1) * out_channels, full * LANES :]
        tail = tail + (pltpu.roll(part, tap * rest, 1) if tap else part)
    tail_ref[...] = tail
    pack_ref[...] = jnp.zeros_like(pack_ref)
    for owner in range(count):
        own = owner * own_rows
        for group in range(full):
            for tap in range(3):
                start = (group * 3 + tap) * own_rows
                row = tap * out_channels + own
                pack_ref[owner % 2, owner // 2, start : start + own_rows, :] = grad_ref[
                    row : row + own_rows, group * LANES : (group + 1) * LANES
                ]
        start = 3 * full * own_rows
        pack_ref[owner % 2, owner // 2, start : start + own_rows, :] = tail_ref[
            own : own + own_rows, :
        ]


VM = pl.BlockSpec(memory_space=pltpu.VMEM)
SM = pl.BlockSpec(memory_space=pltpu.SMEM)


def call(kernel, outs, ins, scratch, flops, args, collective=None):
    extra = {} if collective is None else {"collective_id": collective, "has_side_effects": True}
    return pl.pallas_call(
        kernel,
        out_shape=outs,
        in_specs=ins,
        out_specs=jax.tree.map(lambda _: VM, outs),
        scratch_shapes=scratch,
        cost_estimate=pl.CostEstimate(flops=flops, bytes_accessed=1 << 22, transcendentals=0),
        compiler_params=pltpu.CompilerParams(vmem_limit_bytes=48 * 1024 * 1024, **extra),
    )(*args)


def per_device(features, labels, crop_block, weight, gain, shift, head, run_mean, run_var):
    slab = features[0]
    channels, planes, height, columns = slab.shape
    own_rows = weight.shape[0]
    devices = lax.axis_size("dev")
    roles = lax.axis_size("role")
    own_index = lax.axis_index("dev")
    out_channels = own_rows * devices
    taps = 9 * channels
    blocks = height // CY
    cell_rows = planes * CY
    cells = cell_rows * columns
    table = crop_block[0]
    slots = table.shape[1]
    dims = (planes, blocks, channels, out_channels, columns, slots)
    rows = -(-4 * own_rows // 16) * 16

    own_weight = weight.reshape(own_rows, 9, 3, channels).transpose(2, 0, 1, 3)
    own_weight = own_weight.reshape(3 * own_rows, taps)
    own_weight = jnp.pad(own_weight, ((0, rows - 3 * own_rows), (0, 0)))
    turned = jnp.pad(slab.transpose(1, 2, 0, 3), ((0, 0), (1, 1), (0, 0), (0, 0)))
    turned = turned.reshape(planes, (height + 2) * channels, columns)
    route = lax.dynamic_slice_in_dim(table, own_index, 1, 0)[0]
    live = (table >= 0).astype(F32)
    count = jnp.sum(live, 0) * cells
    counts = jnp.broadcast_to(count[:, None], (slots, LANES))
    live_wide = jnp.broadcast_to(live[:, :, None], live.shape + (LANES,))
    targets = labels[0].reshape(planes, blocks, CY, columns).transpose(1, 0, 2, 3)
    targets = targets.reshape(blocks, cell_rows, columns).astype(F32)

    shape = jax.ShapeDtypeStruct
    conv_flops = 2 * 27 * channels * out_channels * planes * height * columns
    patch = pltpu.VMEM((taps, cells), BF16)
    score_patch = pltpu.VMEM((taps, 8 * columns), BF16)
    tile = pltpu.VMEM((LANES, LANES), F32)
    small = pltpu.VMEM((slots, LANES), F32)
    held = pltpu.VMEM((devices, slots, LANES), F32)
    plane = pltpu.VMEM(turned.shape[1:], BF16)
    signals = pltpu.SemaphoreType.DMA((devices,))
    pair = pltpu.SemaphoreType.DMA((2,))
    params, u, norms, high, scores = call(
        functools.partial(forward_kernel, dims, devices, own_rows),
        (
            shape((4 * out_channels, taps), BF16),
            shape((blocks, out_channels, cells), BF16),
            shape((LANES, LANES), F32),
            shape(turned.shape[1:], BF16),
            shape((planes - 1, height, columns), F32),
        ),
        [SM] * 6 + [VM] * 4,
        [patch, tile, tile, pltpu.VMEM((rows, taps), BF16)]
        + [pltpu.VMEM((devices, rows, taps), BF16), small, held, plane, plane]
        + [signals] * 4
        + [pair] * 2,
        conv_flops * 2,
        (route, gain, shift, head, run_mean, run_var, own_weight, turned, live_wide, counts),
        0,
    )
    sums, vector_terms = call(
        functools.partial(sums_kernel, dims),
        (shape((slots, LANES), F32), shape((out_channels, columns), F32)),
        [SM, SM, VM, VM, VM, VM],
        [tile, tile],
        conv_flops // 16,
        (route, count, params, u, targets, norms),
    )
    means, last_scores = call(
        functools.partial(means_kernel, dims, devices),
        (shape((LANES, LANES), F32), shape((height, columns), F32)),
        [VM] * 5,
        [score_patch, tile, held, signals, signals],
        conv_flops,
        (params, turned, high, sums, counts),
        1,
    )
    full = taps // LANES
    rest = taps - full * LANES
    pack_rows = -(-(3 * full + 1) * own_rows // 8) * 8
    chips = devices // 2
    packed = call(
        functools.partial(grad_kernel, dims),
        shape((2, chips, pack_rows, LANES), F32),
        [SM, SM] + [VM] * 7,
        [patch, pltpu.VMEM((3 * out_channels, cells), BF16)]
        + [pltpu.VMEM((3 * out_channels, (full + 1) * LANES), F32)]
        + [pltpu.VMEM((out_channels, LANES), F32)],
        conv_flops,
        (route, count, params, turned, u, targets, norms, means, vector_terms),
    )
    chunks = pltpu.VMEM((chips, pack_rows, LANES), F32)
    part = pltpu.VMEM((pack_rows, LANES), F32)
    role_signals = pltpu.SemaphoreType.DMA((roles,))
    chip_signals = pltpu.SemaphoreType.DMA((chips,))
    total = call(
        functools.partial(scatter_kernel, devices, roles),
        shape((pack_rows, LANES), F32),
        [VM],
        [chunks, chunks, chunks, part, pltpu.VMEM((roles, pack_rows, LANES), F32)]
        + [pair, pair, chip_signals, chip_signals, role_signals, role_signals],
        conv_flops // 16,
        (packed,),
        2,
    )
    split = 3 * full * own_rows
    front = total[:split].reshape(full, 3, own_rows, LANES).transpose(1, 2, 0, 3)
    back = total[split : split + own_rows]
    sides = back[:, : 3 * rest].reshape(own_rows, 3, rest).transpose(1, 0, 2)
    weight_grad = jnp.concatenate([front.reshape(3, own_rows, full * LANES), sides], 2)
    weight_grad = weight_grad.reshape(3, own_rows, 9, channels).transpose(1, 2, 0, 3)
    weight_grad = weight_grad.reshape(own_rows, 27 * channels)
    vector_grad = back[:, 3 * rest : 3 * rest + 3]
    return jnp.concatenate([scores, last_scores[None]], 0)[None], weight_grad, vector_grad


def solution(mesh):
    in_specs = (
        P("role", None, "dev", None, None),
        P("role", "dev", None, None),
        P("role", None, None),
        P("dev", None),
        P("dev"),
        P("dev"),
        P("dev"),
        P("dev"),
        P("dev"),
    )
    out_specs = (P("role", "dev", None, None), P("dev", None), P("dev", None))
    return jax.shard_map(
        per_device, mesh=mesh, in_specs=in_specs, out_specs=out_specs, check_vma=False
    )
```

```python
import functools

import jax
import jax.numpy as jnp
from jax import lax
from jax.experimental import pallas as pl
from jax.experimental.pallas import tpu as pltpu
from jax.sharding import PartitionSpec as P

CY = 4
EPS = 1e-05
LANES = 128
F32 = jnp.float32
BF16 = jnp.bfloat16


def shift_lanes(value, offset):
    lane = lax.broadcasted_iota(jnp.int32, value.shape, 1)
    width = value.shape[1]
    if offset < 0:
        return jnp.where(lane == 0, 0.0, pltpu.roll(value, 1, 1))
    return jnp.where(lane == width - 1, 0.0, pltpu.roll(value, width - 1, 1))


def column(table, index):
    lane = lax.broadcasted_iota(jnp.int32, table.shape, 1)
    return jnp.sum(jnp.where(lane == index, table, 0.0), axis=1, keepdims=True)


def put_column(ref, rows, index, value):
    part = ref[rows, :]
    lane = lax.broadcasted_iota(jnp.int32, part.shape, 1)
    ref[rows, :] = jnp.where(lane == index, value, part)


def crop_tiles(planes, block, channels):
    for z in range(planes):
        for y in range(CY):
            cell_row = z * CY + y
            for dz in range(3):
                for dy in range(3):
                    zs, ys = z + dz - 1, y + dy - 1
                    if 0 <= zs < planes and 0 <= ys < CY:
                        yield (dz * 3 + dy) * channels, cell_row, zs, ys


def fill_patches(patch_ref, slab_ref, block, planes, channels, columns):
    base = pl.multiple_of((block * CY + 1) * channels, channels)
    for tap_row, cell_row, zs, ys in crop_tiles(planes, block, channels):
        patch_ref[pl.ds(tap_row, channels), pl.ds(cell_row * columns, columns)] = slab_ref[
            zs, pl.ds(base + ys * channels, channels), :
        ]


def conv_rows(weights, patch_ref, first, rows, out_channels, columns):
    taps = jnp.dot(
        weights,
        patch_ref[:, first * columns : (first + rows) * columns],
        preferred_element_type=F32,
    )
    results = []
    for row in range(rows):
        part = taps[:, row * columns : (row + 1) * columns]
        results.append(
            part[out_channels : 2 * out_channels]
            + shift_lanes(part[:out_channels], -1)
            + shift_lanes(part[2 * out_channels :], 1)
        )
    return results


def peer_of(me, step, count):
    return lax.rem(me + step, count)


def greet(axes):
    barrier = pltpu.get_barrier_semaphore()
    total = 0
    for axis, count in axes:
        me = lax.axis_index(axis)

        def tell(step, carry, axis=axis, count=count, me=me):
            pl.semaphore_signal(
                barrier,
                inc=1,
                device_id={axis: peer_of(me, step, count)},
                device_id_type=pl.DeviceIdType.MESH,
            )
            return carry

        lax.fori_loop(1, count, tell, 0)
        total += count - 1
    pl.semaphore_wait(barrier, total)


def to_peer(axis, count, step, source, target, sends, receives):
    me = lax.axis_index(axis)
    peer = peer_of(me, step, count)
    return pltpu.make_async_remote_copy(
        src_ref=source(peer),
        dst_ref=target.at[me],
        send_sem=sends.at[step],
        recv_sem=receives.at[step],
        device_id={axis: peer},
        device_id_type=pl.DeviceIdType.MESH,
    )


def start_all(*parts):
    def one(step, carry):
        to_peer(parts[0], parts[1], step, *parts[2:]).start()
        return carry

    lax.fori_loop(1, parts[1], one, 0)


def wait_all(*parts):
    def one(step, carry):
        to_peer(parts[0], parts[1], step, *parts[2:]).wait()
        return carry

    lax.fori_loop(1, parts[1], one, 0)


def one_hot(rows, columns, target):
    row = lax.broadcasted_iota(jnp.int32, (rows, 1), 0)
    return (lax.broadcasted_iota(jnp.int32, (rows, columns), 1) == target(row)).astype(F32)


def score_plane(dims, z, param_ref, slab_ref, low_ref, high_ref, out_ref, patch):
    planes, blocks, channels, out_channels, columns, slots = dims
    height = blocks * CY
    group = 8
    taps = 3 * channels
    vectors = param_ref[3 * out_channels :, :LANES].astype(F32)
    gain, shift, head, mean, spread = (vectors[:, k : k + 1] for k in range(5))
    inverse = lax.rsqrt(spread + EPS)

    def step(number, carry):
        for row in range(group):
            start = pl.multiple_of((number * group + row) * channels, channels)
            for dz in range(3):
                zs = z + dz - 1
                where = pl.ds(start, taps)
                if zs < 0:
                    piece = low_ref[where, :]
                elif zs >= planes:
                    piece = high_ref[where, :]
                else:
                    piece = slab_ref[zs, where, :]
                patch[dz * taps : (dz + 1) * taps, row * columns : (row + 1) * columns] = piece
        weights = param_ref[0 : 3 * out_channels, :]
        lines = []
        for first in range(0, group, 2):
            for value in conv_rows(weights, patch, first, 2, out_channels, columns):
                hidden = jnp.maximum(gain * ((value - mean) * inverse) + shift, 0.0)
                lines.append(jnp.sum(head * hidden, axis=0, keepdims=True))
        out_ref[pl.ds(pl.multiple_of(number * group, group), group), :] = jnp.concatenate(
            lines, axis=0
        )
        return carry

    lax.fori_loop(0, height // group, step, 0)


def forward_kernel(
    dims,
    count,
    own_rows,
    route_ref,
    gain_ref,
    shift_ref,
    head_ref,
    mean_ref,
    spread_ref,
    weight_ref,
    slab_ref,
    live_ref,
    counts_ref,
    param_ref,
    u_ref,
    norm_ref,
    high_out,
    score_ref,
    patch,
    table,
    turned,
    own,
    held,
    stat,
    stats,
    low,
    high,
    sends,
    receives,
    stat_sends,
    stat_receives,
    halo_sends,
    halo_receives,
):
    planes, blocks, channels, out_channels, columns, slots = dims
    cell_rows = planes * CY
    cells = cell_rows * columns
    me = lax.axis_index("dev")
    rows = own.shape[0]
    tile = weight_ref[...]
    row = lax.broadcasted_iota(jnp.int32, tile.shape, 0)
    lane = lax.broadcasted_iota(jnp.int32, tile.shape, 1)
    for k, ref in enumerate((gain_ref, shift_ref, head_ref, mean_ref, spread_ref)):
        for o in range(own_rows):
            tile = jnp.where((row == 3 * own_rows + o) & (lane == k), ref[o], tile)
    own[...] = tile.astype(BF16)
    greet((("dev", count),))
    exchange = ("dev", count, lambda peer: own, held, sends, receives)
    start_all(*exchange)

    def halo(way):
        return pltpu.make_async_remote_copy(
            src_ref=slab_ref.at[planes - 1 if way == 0 else 0],
            dst_ref=low if way == 0 else high,
            send_sem=halo_sends.at[way],
            recv_sem=halo_receives.at[way],
            device_id={"dev": lax.rem(me + (1 if way == 0 else count - 1), count)},
            device_id_type=pl.DeviceIdType.MESH,
        )

    @pl.when(me < count - 1)
    def _():
        halo(0).start()

    @pl.when(me > 0)
    def _():
        halo(1).start()

    @pl.when(me == 0)
    def _():
        low[...] = jnp.zeros_like(low)

    @pl.when(me == count - 1)
    def _():
        high[...] = jnp.zeros_like(high)

    held[me] = own[...]
    patch[...] = jnp.zeros_like(patch)
    table[...] = jnp.zeros_like(table)
    order = one_hot(
        4 * out_channels,
        count * rows,
        lambda r: (r % out_channels) // own_rows * rows
        + r // out_channels * own_rows
        + r % own_rows,
    ).astype(BF16)
    wait_all(*exchange)

    param_ref[...] = jnp.dot(
        order, held[...].reshape(count * rows, -1), preferred_element_type=F32
    ).astype(BF16)

    def step(block, carry):
        fill_patches(patch, slab_ref, block, planes, channels, columns)
        weights = param_ref[0 : 3 * out_channels, :]
        total = jnp.zeros((out_channels, columns), F32)
        for first in range(0, cell_rows, 2):
            lines = conv_rows(weights, patch, first, 2, out_channels, columns)
            for k, line in enumerate(lines):
                rounded = line.astype(BF16)
                u_ref[block, :, (first + k) * columns : (first + k + 1) * columns] = rounded
                total = total + rounded.astype(F32)
        total = jnp.sum(total, axis=1, keepdims=True)
        mean = total * (1.0 / cells)
        square = jnp.zeros((out_channels, columns), F32)
        for r in range(cell_rows):
            diff = u_ref[block, :, r * columns : (r + 1) * columns].astype(F32) - mean
            square = square + diff * diff
        square = jnp.sum(square, axis=1, keepdims=True)
        put_column(table, slice(0, out_channels), block, total)
        put_column(table, slice(out_channels, 2 * out_channels), block, square)
        return carry

    lax.fori_loop(0, blocks, step, 0)
    turned[...] = jnp.transpose(table[...])

    def route(slot, carry):
        block = route_ref[slot]
        entry = turned[pl.ds(jnp.maximum(block, 0), 1), :]
        stat[pl.ds(slot, 1), :] = jnp.where(block >= 0, entry, 0.0)
        return carry

    lax.fori_loop(0, slots, route, 0)
    exchange = ("dev", count, lambda peer: stat, stats, stat_sends, stat_receives)
    start_all(*exchange)
    stats[me] = stat[...]

    @pl.when(me < count - 1)
    def _():
        halo(0).wait_send()
        halo(1).wait_recv()

    @pl.when(me > 0)
    def _():
        halo(1).wait_send()
        halo(0).wait_recv()

    high_out[...] = high[...]
    score_plane(dims, 0, param_ref, slab_ref, low, high, score_ref.at[0], patch)
    for z in range(1, planes - 1):
        score_plane(dims, z, param_ref, slab_ref, low, high, score_ref.at[z], patch)
    wait_all(*exchange)

    total = stats[0]
    for s in range(1, count):
        total = total + stats[s]
    counts = counts_ref[...]
    mu = total / counts
    spread = jnp.zeros_like(mu)
    for s in range(count):
        entry = stats[s]
        diff = entry * (1.0 / cells) - mu
        spread = spread + (
            pltpu.roll(entry, LANES - out_channels, 1) + live_ref[s] * cells * (diff * diff)
        )
    inverse = lax.rsqrt(spread / counts + EPS)
    wide = lax.broadcasted_iota(jnp.int32, mu.shape, 1)
    table[...] = jnp.zeros_like(table)
    table[0:slots, :] = jnp.where(wide < out_channels, mu, pltpu.roll(inverse, out_channels, 1))
    norm_ref[...] = jnp.transpose(table[...])


def means_kernel(
    dims,
    count,
    param_ref,
    slab_ref,
    high_ref,
    sum_ref,
    counts_ref,
    mean_ref,
    score_ref,
    patch,
    table,
    held,
    sends,
    receives,
):
    planes, slots = dims[0], dims[5]
    greet((("dev", count),))
    exchange = ("dev", count, lambda peer: sum_ref, held, sends, receives)
    start_all(*exchange)
    held[lax.axis_index("dev")] = sum_ref[...]
    score_plane(dims, planes - 1, param_ref, slab_ref, high_ref, high_ref, score_ref, patch)
    wait_all(*exchange)
    total = held[0]
    for s in range(1, count):
        total = total + held[s]
    table[...] = jnp.zeros_like(table)
    table[0:slots, :] = total / counts_ref[...]
    mean_ref[...] = jnp.transpose(table[...])


def scatter_kernel(
    count,
    roles,
    chunk_ref,
    out_ref,
    near,
    mine,
    held,
    part,
    others,
    pair_sends,
    pair_receives,
    sends,
    receives,
    role_sends,
    role_receives,
):
    me = lax.axis_index("dev")
    side, chip, chips = lax.rem(me, 2), lax.div(me, 2), count // 2
    barrier = pltpu.get_barrier_semaphore()

    def tell(**where):
        pl.semaphore_signal(
            barrier, inc=1, device_id=where, device_id_type=pl.DeviceIdType.MESH
        )

    tell(dev=me + 1 - 2 * side)
    for step in range(1, chips):
        tell(dev=lax.rem(chip + step, chips) * 2 + side)
    for step in range(1, roles):
        tell(role=lax.rem(lax.axis_index("role") + step, roles))
    pl.semaphore_wait(barrier, chips + roles - 1)
    swap = pltpu.make_async_remote_copy(
        src_ref=chunk_ref.at[1 - side],
        dst_ref=near,
        send_sem=pair_sends.at[0],
        recv_sem=pair_receives.at[0],
        device_id={"dev": me + 1 - 2 * side},
        device_id_type=pl.DeviceIdType.MESH,
    )
    swap.start()
    swap.wait()
    mine[...] = chunk_ref[side] + near[...]

    def to_chip(step):
        peer = lax.rem(chip + step, chips)
        return pltpu.make_async_remote_copy(
            src_ref=mine.at[peer],
            dst_ref=held.at[chip],
            send_sem=sends.at[step],
            recv_sem=receives.at[step],
            device_id={"dev": peer * 2 + side},
            device_id_type=pl.DeviceIdType.MESH,
        )

    def start(step, carry):
        to_chip(step).start()
        return carry

    def wait(step, carry):
        to_chip(step).wait()
        return carry

    lax.fori_loop(1, chips, start, 0)
    held[chip] = mine[chip]
    lax.fori_loop(1, chips, wait, 0)
    total = held[0]
    for s in range(1, chips):
        total = total + held[s]
    part[...] = total
    exchange = ("role", roles, lambda peer: part, others, role_sends, role_receives)
    start_all(*exchange)
    others[lax.axis_index("role")] = total
    wait_all(*exchange)
    total = others[0]
    for r in range(1, roles):
        total = total + others[r]
    out_ref[...] = total


def crop_row(u_ref, label_ref, block, row, columns, mu, inverse, vectors, count):
    gain, shift, head = vectors
    value = u_ref[block, :, row * columns : (row + 1) * columns].astype(F32)
    normal = (value - mu) * inverse
    before = gain * normal + shift
    hidden = jnp.maximum(before, 0.0)
    score = jnp.sum(head * hidden, axis=0, keepdims=True)
    residual = (score - label_ref[block, row : row + 1, :]) / count
    dbefore = jnp.where(before > 0, head * residual, 0.0)
    return normal, hidden, residual, dbefore


def sums_kernel(
    dims,
    route_ref,
    count_ref,
    param_ref,
    u_ref,
    label_ref,
    norm_ref,
    sum_ref,
    vec_ref,
    square,
    table,
):
    planes, blocks, channels, out_channels, columns, slots = dims
    cell_rows = planes * CY
    table[...] = jnp.zeros_like(table)
    vec_ref[...] = jnp.zeros_like(vec_ref)

    def step(slot, carry):
        block = route_ref[slot]

        @pl.when(block >= 0)
        def _():
            vec = param_ref[3 * out_channels :, :LANES].astype(F32)
            vectors = tuple(vec[:, k : k + 1] for k in range(3))
            pair = column(norm_ref[...], slot)
            mean, inv = pair[:out_channels], pair[out_channels:]
            cell_count = count_ref[slot]
            first = jnp.zeros((out_channels, columns), F32)
            second, third = first, first
            for row in range(cell_rows):
                normal, hidden, residual, dbefore = crop_row(
                    u_ref, label_ref, block, row, columns, mean, inv, vectors, cell_count
                )
                first = first + dbefore
                second = second + dbefore * normal
                third = third + hidden * residual
            put_column(
                table, slice(0, out_channels), slot, jnp.sum(first, axis=1, keepdims=True)
            )
            put_column(
                table,
                slice(out_channels, 2 * out_channels),
                slot,
                jnp.sum(second, axis=1, keepdims=True),
            )
            vec_ref[...] += third

        return carry

    lax.fori_loop(0, slots, step, 0)
    both = table[...]
    sums = jnp.sum(both, axis=1, keepdims=True)
    last = jnp.sum(vec_ref[...], axis=1, keepdims=True)
    wide = lax.broadcasted_iota(jnp.int32, vec_ref.shape, 1)
    vec_ref[...] = jnp.where(
        wide == 0,
        sums[out_channels:],
        jnp.where(wide == 1, sums[:out_channels], jnp.where(wide == 2, last, 0.0)),
    )
    square[...] = jnp.transpose(both)
    sum_ref[...] = square[0:slots, :]


def grad_kernel(
    dims,
    route_ref,
    count_ref,
    param_ref,
    slab_ref,
    u_ref,
    label_ref,
    norm_ref,
    means,
    vec_ref,
    pack_ref,
    patch,
    field,
    grad_ref,
    tail_ref,
):
    planes, blocks, channels, out_channels, columns, slots = dims
    cell_rows = planes * CY
    count = 2 * pack_ref.shape[1]
    own_rows = out_channels // count
    taps = 9 * channels
    patch[...] = jnp.zeros_like(patch)
    grad_ref[...] = jnp.zeros_like(grad_ref)

    def step(slot, carry):
        block = route_ref[slot]

        @pl.when(block >= 0)
        def _():
            vec = param_ref[3 * out_channels :, :LANES].astype(F32)
            vectors = tuple(vec[:, k : k + 1] for k in range(3))
            gain = vectors[0]
            pair = column(norm_ref[...], slot)
            mean, inv = pair[:out_channels], pair[out_channels:]
            pair = column(means[...], slot)
            first, second = gain * pair[:out_channels], gain * pair[out_channels:]
            cell_count = count_ref[slot]
            fill_patches(patch, slab_ref, block, planes, channels, columns)
            for row in range(cell_rows):
                normal, hidden, residual, dbefore = crop_row(
                    u_ref, label_ref, block, row, columns, mean, inv, vectors, cell_count
                )
                du = inv * (dbefore * gain - first - normal * second)
                du = du.astype(BF16).astype(F32)
                where = slice(row * columns, (row + 1) * columns)
                field[0:out_channels, where] = shift_lanes(du, 1).astype(BF16)
                field[out_channels : 2 * out_channels, where] = du.astype(BF16)
                field[2 * out_channels :, where] = shift_lanes(du, -1).astype(BF16)
            grad_ref[:, 0:taps] += lax.dot_general(
                field[...], patch[...], (((1,), (1,)), ((), ())), preferred_element_type=F32
            )

        return carry

    lax.fori_loop(0, slots, step, 0)
    full = taps // LANES
    rest = taps - full * LANES
    tail = pltpu.roll(vec_ref[...], 3 * rest, 1)
    for tap in range(3):
        part = grad_ref[tap * out_channels : (tap + 1) * out_channels, full * LANES :]
        tail = tail + (pltpu.roll(part, tap * rest, 1) if tap else part)
    tail_ref[...] = tail
    pack_ref[...] = jnp.zeros_like(pack_ref)
    for owner in range(count):
        own = owner * own_rows
        for group in range(full):
            for tap in range(3):
                start = (group * 3 + tap) * own_rows
                row = tap * out_channels + own
                pack_ref[owner % 2, owner // 2, start : start + own_rows, :] = grad_ref[
                    row : row + own_rows, group * LANES : (group + 1) * LANES
                ]
        start = 3 * full * own_rows
        pack_ref[owner % 2, owner // 2, start : start + own_rows, :] = tail_ref[
            own : own + own_rows, :
        ]


VM = pl.BlockSpec(memory_space=pltpu.VMEM)
SM = pl.BlockSpec(memory_space=pltpu.SMEM)


def call(kernel, outs, ins, scratch, flops, args, collective=None):
    extra = {} if collective is None else {"collective_id": collective, "has_side_effects": True}
    return pl.pallas_call(
        kernel,
        out_shape=outs,
        in_specs=ins,
        out_specs=jax.tree.map(lambda _: VM, outs),
        scratch_shapes=scratch,
        cost_estimate=pl.CostEstimate(flops=flops, bytes_accessed=1 << 22, transcendentals=0),
        compiler_params=pltpu.CompilerParams(vmem_limit_bytes=48 * 1024 * 1024, **extra),
    )(*args)


def per_device(features, labels, crop_block, weight, gain, shift, head, run_mean, run_var):
    slab = features[0]
    channels, planes, height, columns = slab.shape
    own_rows = weight.shape[0]
    devices = lax.axis_size("dev")
    roles = lax.axis_size("role")
    own_index = lax.axis_index("dev")
    out_channels = own_rows * devices
    taps = 9 * channels
    blocks = height // CY
    cell_rows = planes * CY
    cells = cell_rows * columns
    table = crop_block[0]
    slots = table.shape[1]
    dims = (planes, blocks, channels, out_channels, columns, slots)
    rows = -(-4 * own_rows // 16) * 16

    own_weight = weight.reshape(own_rows, 9, 3, channels).transpose(2, 0, 1, 3)
    own_weight = own_weight.reshape(3 * own_rows, taps)
    own_weight = jnp.pad(own_weight, ((0, rows - 3 * own_rows), (0, 0)))
    turned = jnp.pad(slab.transpose(1, 2, 0, 3), ((0, 0), (1, 1), (0, 0), (0, 0)))
    turned = turned.reshape(planes, (height + 2) * channels, columns)
    route = lax.dynamic_slice_in_dim(table, own_index, 1, 0)[0]
    live = (table >= 0).astype(F32)
    count = jnp.sum(live, 0) * cells
    counts = jnp.broadcast_to(count[:, None], (slots, LANES))
    live_wide = jnp.broadcast_to(live[:, :, None], live.shape + (LANES,))
    targets = labels[0].reshape(planes, blocks, CY, columns).transpose(1, 0, 2, 3)
    targets = targets.reshape(blocks, cell_rows, columns).astype(F32)

    shape = jax.ShapeDtypeStruct
    conv_flops = 2 * 27 * channels * out_channels * planes * height * columns
    patch = pltpu.VMEM((taps, cells), BF16)
    score_patch = pltpu.VMEM((taps, 8 * columns), BF16)
    tile = pltpu.VMEM((LANES, LANES), F32)
    small = pltpu.VMEM((slots, LANES), F32)
    held = pltpu.VMEM((devices, slots, LANES), F32)
    plane = pltpu.VMEM(turned.shape[1:], BF16)
    signals = pltpu.SemaphoreType.DMA((devices,))
    pair = pltpu.SemaphoreType.DMA((2,))
    params, u, norms, high, scores = call(
        functools.partial(forward_kernel, dims, devices, own_rows),
        (
            shape((4 * out_channels, taps), BF16),
            shape((blocks, out_channels, cells), BF16),
            shape((LANES, LANES), F32),
            shape(turned.shape[1:], BF16),
            shape((planes - 1, height, columns), F32),
        ),
        [SM] * 6 + [VM] * 4,
        [patch, tile, tile, pltpu.VMEM((rows, taps), BF16)]
        + [pltpu.VMEM((devices, rows, taps), BF16), small, held, plane, plane]
        + [signals] * 4
        + [pair] * 2,
        conv_flops * 2,
        (route, gain, shift, head, run_mean, run_var, own_weight, turned, live_wide, counts),
        0,
    )
    sums, vector_terms = call(
        functools.partial(sums_kernel, dims),
        (shape((slots, LANES), F32), shape((out_channels, columns), F32)),
        [SM, SM, VM, VM, VM, VM],
        [tile, tile],
        conv_flops // 16,
        (route, count, params, u, targets, norms),
    )
    means, last_scores = call(
        functools.partial(means_kernel, dims, devices),
        (shape((LANES, LANES), F32), shape((height, columns), F32)),
        [VM] * 5,
        [score_patch, tile, held, signals, signals],
        conv_flops,
        (params, turned, high, sums, counts),
        1,
    )
    full = taps // LANES
    rest = taps - full * LANES
    pack_rows = -(-(3 * full + 1) * own_rows // 8) * 8
    chips = devices // 2
    packed = call(
        functools.partial(grad_kernel, dims),
        shape((2, chips, pack_rows, LANES), F32),
        [SM, SM] + [VM] * 7,
        [patch, pltpu.VMEM((3 * out_channels, cells), BF16)]
        + [pltpu.VMEM((3 * out_channels, (full + 1) * LANES), F32)]
        + [pltpu.VMEM((out_channels, LANES), F32)],
        conv_flops,
        (route, count, params, turned, u, targets, norms, means, vector_terms),
    )
    chunks = pltpu.VMEM((chips, pack_rows, LANES), F32)
    part = pltpu.VMEM((pack_rows, LANES), F32)
    role_signals = pltpu.SemaphoreType.DMA((roles,))
    chip_signals = pltpu.SemaphoreType.DMA((chips,))
    total = call(
        functools.partial(scatter_kernel, devices, roles),
        shape((pack_rows, LANES), F32),
        [VM],
        [chunks, chunks, chunks, part, pltpu.VMEM((roles, pack_rows, LANES), F32)]
        + [pair, pair, chip_signals, chip_signals, role_signals, role_signals],
        conv_flops // 16,
        (packed,),
        2,
    )
    split = 3 * full * own_rows
    front = total[:split].reshape(full, 3, own_rows, LANES).transpose(1, 2, 0, 3)
    back = total[split : split + own_rows]
    sides = back[:, : 3 * rest].reshape(own_rows, 3, rest).transpose(1, 0, 2)
    weight_grad = jnp.concatenate([front.reshape(3, own_rows, full * LANES), sides], 2)
    weight_grad = weight_grad.reshape(3, own_rows, 9, channels).transpose(1, 2, 0, 3)
    weight_grad = weight_grad.reshape(own_rows, 27 * channels)
    vector_grad = back[:, 3 * rest : 3 * rest + 3]
    return jnp.concatenate([scores, last_scores[None]], 0)[None], weight_grad, vector_grad


def solution(mesh):
    in_specs = (
        P("role", None, "dev", None, None),
        P("role", "dev", None, None),
        P("role", None, None),
        P("dev", None),
        P("dev"),
        P("dev"),
        P("dev"),
        P("dev"),
        P("dev"),
    )
    out_specs = (P("role", "dev", None, None), P("dev", None), P("dev", None))
    return jax.shard_map(
        per_device, mesh=mesh, in_specs=in_specs, out_specs=out_specs, check_vma=False
    )
```
